128 devices in a mesh: row: 8 (over z, x_hi), col: 16 (over y, x_lo, core).
Axes of the slice: x: 4 (x_hi: 2, x_lo: 2; x = x_hi * 2 + x_lo), y: 4, z: 4, core: 2. Of those that a mesh axis runs over, the one named last changes fastest.
Arguments:
- embed: bfloat16 [32768, 768], P(('row', 'col')), as said below
- cand_tiles: int32 [256], P(('row', 'col')), may hold values from 0 to 7
Outputs:
- counts: float32 [32768], P(('row', 'col'))
- tops: float32 [32768], P(('row', 'col'))
- recount: float32 [256, 256], P(('row', 'col'))
The draws below stay inside these ranges and needn't reach their ends.
Inputs may be any that keep to these rules, and one draw needn't show every extreme that they name: Rows of embed have norms near 1.
All inputs are finite; a program needn't handle non-finite values.
Results may differ from the reference program's by a relative error of at most 0.0008.
Values may be sent and summed in bfloat16 or wider, within the bound.
A program may use at most 64 MiB of HBM per device.

```python
import math
import jax
import jax.numpy as jnp
from jax import lax

D = 768
ROWS_DEV = 256
CAND_DEV = 2
ROWS = 32768
CANDS = 256
N_ROW = 8
N_COL = 16


def draw_embed(key, part):
    key = jax.random.fold_in(key, 11)
    key_ids, key_centers, key_noise, key_mix = jax.random.split(key, 4)
    groups = ROWS // 8
    member = jax.random.randint(key_ids, (ROWS,), 0, groups)
    centers = jax.random.normal(key_centers, (groups, D), jnp.float32)
    noise = jax.random.normal(key_noise, (ROWS, D), jnp.float32)
    mix = jax.random.uniform(key_mix, (ROWS, 1), jnp.float32, 0.78, 0.95)
    mixed = jnp.sqrt(mix) * jnp.take(centers, member, axis=0) + jnp.sqrt(1.0 - mix) * noise
    return (mixed / jnp.sqrt(jnp.float32(D))).astype(jnp.bfloat16)


def touch_ends(values, own_key, least, largest):
    shape = values.shape
    spot = [jax.random.randint(jax.random.fold_in(own_key, axis), (), 0, shape[axis]) for axis in range(len(shape))]
    values = values.at[tuple(spot)].set(least)
    longest = shape.index(max(shape))
    spot[longest] = (spot[longest] + 1) % shape[longest]
    return values.at[tuple(spot)].set(largest)


def setup_inputs(seed: int = 0) -> dict:
    streams_of = jax.random.split(jax.random.key(seed), 3)
    return {
        "embed": draw_embed(jax.random.fold_in(streams_of[2], 71), 0),
        "cand_tiles": touch_ends(jax.random.randint(streams_of[1], (CANDS,), 0, N_ROW), jax.random.fold_in(streams_of[1], 1), 0, N_ROW - 1).astype(jnp.int32),
    }


def reference(embed, cand_tiles):
    total_rows = embed.shape[0]
    block = math.gcd(total_rows, 512)
    columns = jnp.arange(total_rows, dtype=jnp.int32)

    def one_block(first):
        rows_here = lax.dynamic_slice_in_dim(embed, first, block, 0)
        scores = lax.dot_general(rows_here, embed, (((1,), (1,)), ((), ())), preferred_element_type=jnp.float32)
        ids = first + jnp.arange(block, dtype=jnp.int32)
        itself = ids[:, None] == columns[None, :]
        sums = jnp.sum(jnp.where(itself, jnp.float32(0.0), jnp.exp(20.0 * (scores - 1.0))), axis=1)
        highs = jnp.max(jnp.where(itself, jnp.float32(-3.0), scores), axis=1)
        return sums, highs

    starts = jnp.arange(0, total_rows, block, dtype=jnp.int32)
    sums, highs = lax.map(one_block, starts)
    counts = sums.reshape(total_rows)
    tops = highs.reshape(total_rows)

    diagonal_mask = jnp.eye(ROWS_DEV, dtype=jnp.bool_)

    def one_candidate(number):
        owner = number // CAND_DEV
        other = N_COL * cand_tiles[number] + owner % N_COL
        left = lax.dynamic_slice_in_dim(embed, (owner * ROWS_DEV).astype(jnp.int32), ROWS_DEV, 0)
        right = lax.dynamic_slice_in_dim(embed, (other * ROWS_DEV).astype(jnp.int32), ROWS_DEV, 0)
        scores = lax.dot_general(left, right, (((1,), (1,)), ((), ())), preferred_element_type=jnp.float32)
        itself = jnp.logical_and(diagonal_mask, other == owner)
        return jnp.sum(jnp.where(itself, jnp.float32(0.0), jnp.exp(20.0 * (scores - 1.0))), axis=1)

    recount = lax.map(one_candidate, jnp.arange(cand_tiles.shape[0], dtype=jnp.int32))
    return counts, tops, recount
```

```python
import jax
import jax.numpy as jnp
from jax import lax
from jax.experimental import pallas as pl
from jax.experimental.pallas import tpu as pltpu
from jax.sharding import PartitionSpec as P

MESH = pl.DeviceIdType.MESH
ROWS = 256
WIDTH = 768
SCALE = 20.0 * 1.4426950408889634
LOWEST = -3.0
TRANSPOSED = (((1,), (1,)), ((), ()))
DIRECTIONS = ((1, 0, 0), (3, 0, 0), (0, 1, 0), (0, 3, 0), (0, 0, 1), (0, 0, 3))
CHUNKS = 4
TILES = (
   (0, 0, 0),
   (0, 0, 1),
   (0, 0, 2),
   (0, 0, 3),
   (0, 1, 0),
   (0, 2, 0),
   (1, 0, 2),
   (1, 0, 3),
   (2, 2, 0),
   (2, 3, 0),
   (3, 0, 0),
   (3, 3, 0),
)
ROUTES = (
    (),
   (4, 4, 4, 4),
   (4, 5, 4, 4),
   (5, 5, 5, 5),
   (2, 2, 2, 2),
   (2, 2, 2, 2),
   (0, 0, 5, 5),
   (0, 0, 0, 0),
   (3, 3, 3, 3),
   (1, 1, 1, 1),
   (1, 1, 1, 1),
   (3, 3, 3, 3),
)
PAIRS = (
   (4, 0, 0),
   (1, 0, 0),
   (10, 0, 0),
   (1, 3, 1),
   (3, 4, 0),
   (1, 4, 0),
   (1, 10, 0),
   (3, 10, 0),
   (4, 10, 0),
   (11, 4, 0),
   (7, 10, 0),
   (7, 4, 0),
   (11, 3, 0),
   (11, 1, 0),
   (7, 1, 0),
   (7, 11, 0),
   (2, 11, 0),
   (2, 4, 0),
   (6, 11, 0),
   (6, 10, 1),
   (6, 4, 0),
   (5, 0, 1),
   (9, 4, 1),
   (9, 1, 0),
   (9, 0, 0),
   (9, 7, 0),
   (5, 11, 0),
   (5, 7, 0),
   (5, 1, 0),
   (5, 2, 1),
   (5, 6, 0),
   (8, 5, 1),
   (8, 7, 0),
   (8, 1, 0),
   (8, 2, 1),
)
ARRIVALS = (
    ((1, 0), (3, 0), (4, 0), (10, 0), (1, 1), (3, 1), (4, 1), (10, 1), (7, 0), (11, 0), (1, 2), (3, 2), (4, 2), (10, 2), (7, 1), (11, 1), (1, 3), (3, 3), (4, 3), (10, 3),),
    ((7, 2), (11, 2),),
    (),
    ((2, 0), (2, 1), (5, 0), (9, 0),),
    ((7, 3), (11, 3),),
    (),
    ((2, 2), (5, 1), (9, 1), (6, 2),),
    (),
    ((6, 0), (8, 0), (2, 3), (5, 2), (9, 2), (6, 3),),
    ((6, 1), (8, 1),),
    ((5, 3), (9, 3),),
    (),
    ((8, 2),),
    (),
    (),
    ((8, 3),),
    (),
    (),
)
COUNT = len(TILES)
PIECE = ROWS // CHUNKS


def minus(a, b):
    return tuple((p - q) % 4 for p, q in zip(a, b))


def parent(tile, chunk):
    return TILES.index(minus(TILES[tile], DIRECTIONS[ROUTES[tile][chunk]]))


def children():
    table = {}
    for tile in range(1, COUNT):
        for chunk in range(CHUNKS):
            table.setdefault((parent(tile, chunk), chunk), []).append((tile, chunk))
    return table


CHILDREN = children()
ROW_TILES = sorted({x for x, _, _ in PAIRS})
SHARED_TILES = sorted({y for _, y, _ in PAIRS} | {0})
COL_TILES = sorted({y for _, y, one in PAIRS if not one})


def kept_rows():
    kept = []
    fill = [2] * COUNT
    for number, (x, y, one) in enumerate(PAIRS):
        apart = minus(TILES[y], TILES[x])
        if apart[1] == 0 and apart[0] % 2 == 0:
            back = minus(TILES[x], TILES[y])
            left = (x, fill[x], apart[2] * 2 + apart[0] // 2)
            fill[x] += 1
            right = None
            if not one:
                right = (y, fill[y], back[2] * 2 + back[0] // 2)
                fill[y] += 1
            kept.append((number, left, right))
    return kept


KEPT = kept_rows()
KEPT_OF = {number: place for place, (number, _, _) in enumerate(KEPT)}
SPARE_ROW = COUNT
SPARE_KEPT = len(KEPT)
SPARE_COL = COUNT
KEPT_COL = COUNT + 1


def slots(number):
    x, y, one = PAIRS[number]
    kept = KEPT_OF.get(number, SPARE_KEPT)
    if one:
        col = SPARE_COL
    elif kept != SPARE_KEPT:
        col = KEPT_COL + kept
    else:
        col = y
    return (x, y, x, kept, col)


NOTHING = (0, 0, SPARE_ROW, SPARE_KEPT, SPARE_COL)
ROUNDS = (len(PAIRS) + 1) // 2


def first_use(tile):
    for number, (_, y, _) in enumerate(PAIRS):
        if y == tile:
            return number // 2
    return None


def kernel(
    cand_ref, embed_ref, counts_ref, tops_ref, recount_ref,
    tiles, near, far, row_sums, row_tops, kept_sums, col_sums, col_tops,
    outbox, inbox, table,
    own_sem, hop_send, hop_recv, twin_send, twin_recv, post_send, post_recv,
):
    my_row = lax.axis_index("row")
    my_col = lax.axis_index("col")
    z, x_hi = my_row // 2, my_row % 2
    y, x_lo, core = my_col // 4, (my_col // 2) % 2, my_col % 2
    x = x_hi * 2 + x_lo
    other = 1 - core

    def device(offset, at_core):
        px = (x + offset[0]) % 4
        py = (y + offset[1]) % 4
        pz = (z + offset[2]) % 4
        return (pz * 2 + px // 2, py * 4 + (px % 2) * 2 + at_core)

    def span(chunk):
        return pl.ds(chunk * PIECE, PIECE)

    def hop(tile, chunk):
        origin = parent(tile, chunk)
        step = DIRECTIONS[ROUTES[tile][chunk]]
        source = embed_ref.at[span(chunk)] if origin == 0 else tiles.at[origin, core, span(chunk)]
        return pltpu.make_async_remote_copy(
            src_ref=source,
            dst_ref=tiles.at[tile, core, span(chunk)],
            send_sem=hop_send.at[tile, chunk],
            recv_sem=hop_recv.at[tile, chunk],
            device_id=device(minus((0, 0, 0), step), core),
            device_id_type=MESH,
        )

    def twin(tile, chunk):
        source = embed_ref.at[span(chunk)] if tile == 0 else tiles.at[tile, core, span(chunk)]
        return pltpu.make_async_remote_copy(
            src_ref=source,
            dst_ref=tiles.at[tile, core, span(chunk)],
            send_sem=twin_send.at[tile],
            recv_sem=twin_recv.at[tile],
            device_id=device((0, 0, 0), other),
            device_id_type=MESH,
        )

    def twin_whole(tile):
        return pltpu.make_async_remote_copy(
            src_ref=tiles.at[tile, other],
            dst_ref=tiles.at[tile, other],
            send_sem=twin_send.at[tile],
            recv_sem=twin_recv.at[tile],
            device_id=device((0, 0, 0), other),
            device_id_type=MESH,
        )

    def post(tile, at_core):
        return pltpu.make_async_remote_copy(
            src_ref=outbox.at[tile, at_core],
            dst_ref=inbox.at[tile, core],
            send_sem=post_send.at[tile, at_core],
            recv_sem=post_recv.at[tile, core],
            device_id=device(TILES[tile], at_core),
            device_id_type=MESH,
        )

    def posted(tile, from_core):
        return pltpu.make_async_remote_copy(
            src_ref=outbox.at[tile, from_core],
            dst_ref=inbox.at[tile, from_core],
            send_sem=post_send.at[tile, from_core],
            recv_sem=post_recv.at[tile, from_core],
            device_id=device(TILES[tile], from_core),
            device_id_type=MESH,
        )

    own = pltpu.make_async_copy(embed_ref, tiles.at[0, core], own_sem)
    own.start()

    barrier = pltpu.get_barrier_semaphore()
    for step in DIRECTIONS:
        pl.semaphore_signal(barrier, inc=1, device_id=device(step, core), device_id_type=MESH)
    pl.semaphore_signal(barrier, inc=1, device_id=device((0, 0, 0), other), device_id_type=MESH)
    pl.semaphore_wait(barrier, 7)

    for chunk in range(CHUNKS):
        for tile, piece in CHILDREN.get((0, chunk), ()):
            hop(tile, piece).start()
    for chunk in range(CHUNKS):
        twin(0, chunk).start()

    row_sums[...] = jnp.zeros_like(row_sums)
    col_sums[...] = jnp.zeros_like(col_sums)
    row_tops[...] = jnp.full_like(row_tops, LOWEST)
    col_tops[...] = jnp.full_like(col_tops, LOWEST)
    far[...] = jnp.zeros_like(far)

    def multiply(target, left, right):
        target[...] = lax.dot_general(
            tiles[left, core], tiles[right].reshape(2 * ROWS, WIDTH), TRANSPOSED,
            preferred_element_type=jnp.float32,
        )

    def halves(op, values):
        return (
            op(values[:, 0:128], values[:, 128:256]),
            op(values[:, 256:384], values[:, 384:512]),
        )

    def reduce(source, row, kept, col, own_pair=False):
        sums = tops = None
        for first in range(0, ROWS, 64):
            part = pl.ds(first, 64)
            scores = source[part, :]
            weights = jnp.exp2(scores * SCALE - SCALE)
            if own_pair:
                place = lax.broadcasted_iota(jnp.int32, (64, 2 * ROWS), 0) + (first + core * ROWS)
                itself = place == lax.broadcasted_iota(jnp.int32, (64, 2 * ROWS), 1)
                weights = jnp.where(itself, 0.0, weights)
                scores = jnp.where(itself, LOWEST, scores)
            left, right = halves(jnp.add, weights)
            row_sums[row, part] += left + right
            kept_sums[kept, part] = jnp.where(core == 0, left, right)
            row_tops[row, part] = jnp.maximum(
                row_tops[row, part], jnp.maximum(*halves(jnp.maximum, scores))
            )
            if own_pair:
                continue
            for at in range(0, 64, 8):
                sums = weights[at:at + 8] if sums is None else sums + weights[at:at + 8]
                high = scores[at:at + 8]
                tops = high if tops is None else jnp.maximum(tops, high)
        if not own_pair:
            col_sums[col] += sums
            col_tops[col] = jnp.maximum(col_tops[col], tops)

    def arrive(tile, chunk):
        hop(tile, chunk).wait_recv()
        for child, piece in CHILDREN.get((tile, chunk), ()):
            hop(child, piece).start()
        if tile in SHARED_TILES:
            twin(tile, chunk).start()

    own.wait()
    twin_whole(0).wait_recv()
    multiply(near, 0, 0)
    reduce(near, 0, SPARE_KEPT + 1, SPARE_COL, own_pair=True)

    def arrivals(number):
        def run():
            for tile, chunk in ARRIVALS[number]:
                arrive(tile, chunk)
            for tile in SHARED_TILES:
                if tile != 0 and first_use(tile) == number:
                    twin_whole(tile).wait_recv()
            values = []
            for step in (2 * number, 2 * number + 1):
                values += slots(step) if step < len(PAIRS) else NOTHING
            return tuple(jnp.int32(v) for v in values)
        return run

    def round_of(number, before):
        now = lax.switch(number, [arrivals(n) for n in range(ROUNDS)])
        multiply(near, now[0], now[1])
        reduce(far, *before)
        multiply(far, now[5], now[6])
        reduce(near, *now[2:5])
        return tuple(now[7:10])

    last = lax.fori_loop(
        0, ROUNDS, round_of, tuple(jnp.int32(v) for v in NOTHING[2:5])
    )
    reduce(far, *last)

    def across(values, op):
        return op(values.T, axis=0, keepdims=True)

    sends = []
    for tile in list(range(1, COUNT)) + [0]:
        for at_core in (0, 1):
            lanes = pl.ds(at_core * ROWS, ROWS)
            sums = jnp.zeros((1, ROWS), jnp.float32)
            tops = jnp.full((1, ROWS), LOWEST, jnp.float32)
            if tile in COL_TILES:
                sums = jnp.sum(col_sums[tile, :, lanes], axis=0, keepdims=True)
                tops = jnp.max(col_tops[tile, :, lanes], axis=0, keepdims=True)
            for place, (_, _, right) in enumerate(KEPT):
                if right is not None and right[0] == tile:
                    extra = jnp.sum(col_sums[KEPT_COL + place, :, lanes], axis=0, keepdims=True)
                    sums = sums + extra
                    outbox[tile, at_core, pl.ds(right[1], 1), :] = extra
                    tops = jnp.maximum(
                        tops, jnp.max(col_tops[KEPT_COL + place, :, lanes], axis=0, keepdims=True)
                    )
            outbox[tile, at_core, 0:1, :] = sums
            outbox[tile, at_core, 1:2, :] = tops
        if tile in ROW_TILES or tile == 0:
            outbox[tile, core, 0:1, :] += across(row_sums[tile], jnp.sum)
            outbox[tile, core, 1:2, :] = jnp.maximum(
                outbox[tile, core, 1:2, :], across(row_tops[tile], jnp.max)
            )
        for place, (_, left, _) in enumerate(KEPT):
            if left[0] == tile:
                outbox[tile, core, pl.ds(left[1], 1), :] = across(kept_sums[place], jnp.sum)
        if tile != 0:
            post(tile, core).start()
        if tile in COL_TILES:
            post(tile, other).start()
    table[0:1, :] = across(kept_sums[SPARE_KEPT + 1], jnp.sum)

    sums = outbox[0, core, 0:1, :]
    tops = outbox[0, core, 1:2, :]
    for tile in list(range(1, COUNT)) + [0]:
        for from_core in (core, other):
            if from_core is core and tile == 0:
                continue
            if from_core is other and tile not in COL_TILES:
                continue
            posted(tile, from_core).wait_recv()
            sums = sums + inbox[tile, from_core, 0:1, :]
            tops = jnp.maximum(tops, inbox[tile, from_core, 1:2, :])
    counts_ref[...] = sums
    tops_ref[...] = tops
    for _, left, right in KEPT:
        for side in (left, right):
            if side is not None:
                where = outbox if side[0] == 0 else inbox
                table[pl.ds(side[2], 1), :] = where[side[0], core, pl.ds(side[1], 1), :]
    for number in range(2):
        chosen = cand_ref[number]
        apart = ((chosen // 2 - z + 4) % 4) * 2 + (chosen % 2 - x_hi + 2) % 2
        recount_ref[pl.ds(number, 1), :] = table[pl.ds(apart, 1), :]

    for tile in range(1, COUNT):
        for chunk in range(CHUNKS):
            hop(tile, chunk).wait_send()
    for tile in SHARED_TILES:
        twin_whole(tile).wait_send()
    for tile in range(COUNT):
        if tile != 0:
            post(tile, core).wait_send()
        if tile in COL_TILES:
            post(tile, other).wait_send()


def per_device(embed, cand_tiles):
    vector = pltpu.VMEM
    semaphores = pltpu.SemaphoreType.DMA
    counts, tops, recount = pl.pallas_call(
        kernel,
        out_shape=(
            jax.ShapeDtypeStruct((1, ROWS), jnp.float32),
            jax.ShapeDtypeStruct((1, ROWS), jnp.float32),
            jax.ShapeDtypeStruct((2, ROWS), jnp.float32),
        ),
        in_specs=[
            pl.BlockSpec(memory_space=pltpu.SMEM),
            pl.BlockSpec(memory_space=pl.ANY),
        ],
        out_specs=[pl.BlockSpec(memory_space=pltpu.VMEM)] * 3,
        scratch_shapes=[
            vector((COUNT, 2, ROWS, WIDTH), jnp.bfloat16),
            vector((ROWS, 2 * ROWS), jnp.float32),
            vector((ROWS, 2 * ROWS), jnp.float32),
            vector((COUNT + 1, ROWS, 128), jnp.float32),
            vector((COUNT + 1, ROWS, 128), jnp.float32),
            vector((SPARE_KEPT + 2, ROWS, 128), jnp.float32),
            vector((KEPT_COL + len(KEPT), 8, 2 * ROWS), jnp.float32),
            vector((KEPT_COL + len(KEPT), 8, 2 * ROWS), jnp.float32),
            vector((COUNT, 2, 8, ROWS), jnp.float32),
            vector((COUNT, 2, 8, ROWS), jnp.float32),
            vector((8, ROWS), jnp.float32),
            semaphores,
            semaphores((COUNT, CHUNKS)),
            semaphores((COUNT, CHUNKS)),
            semaphores((COUNT,)),
            semaphores((COUNT,)),
            semaphores((COUNT, 2)),
            semaphores((COUNT, 2)),
        ],
        compiler_params=pltpu.CompilerParams(
            collective_id=0, has_side_effects=True, vmem_limit_bytes=56 * 1024 * 1024
        ),
        cost_estimate=pl.CostEstimate(
            flops=37 * 2 * ROWS * 2 * ROWS * WIDTH,
            bytes_accessed=COUNT * 2 * ROWS * WIDTH * 2,
            transcendentals=37 * ROWS * 2 * ROWS,
        ),
    )(cand_tiles, embed)
    return counts.reshape(ROWS), tops.reshape(ROWS), recount


def solution(mesh):
    in_specs = (P(("row", "col"), None), P(("row", "col")))
    out_specs = (P(("row", "col")), P(("row", "col")), P(("row", "col"), None))
    return jax.shard_map(
        per_device, mesh=mesh, in_specs=in_specs, out_specs=out_specs, check_vma=False
    )
```

```python
import jax
import jax.numpy as jnp
from jax import lax
from jax.experimental import pallas as pl
from jax.experimental.pallas import tpu as pltpu
from jax.sharding import PartitionSpec as P

MESH = pl.DeviceIdType.MESH
ROWS = 256
WIDTH = 768
SCALE = 20.0 * 1.4426950408889634
LOWEST = -3.0
TRANSPOSED = (((1,), (1,)), ((), ()))
DIRECTIONS = ((1, 0, 0), (3, 0, 0), (0, 1, 0), (0, 3, 0), (0, 0, 1), (0, 0, 3))
CHUNKS = 4
TILES = (
   (0, 0, 0),
   (0, 0, 3),
   (0, 1, 2),
   (0, 1, 3),
   (0, 2, 0),
   (0, 2, 2),
   (0, 3, 0),
   (1, 0, 0),
   (2, 0, 0),
   (2, 0, 1),
   (3, 0, 0),
   (3, 0, 1),
)
ROUTES = (
    (),
   (5, 5, 5, 5),
   (5, 5, 5, 5),
   (2, 2, 2, 2),
   (3, 3, 3, 3),
   (2, 2, 2, 2),
   (3, 3, 3, 3),
   (0, 0, 0, 0),
   (0, 0, 5, 0),
   (1, 1, 1, 4),
   (1, 1, 1, 1),
   (4, 4, 4, 4),
)
FIRST = ((1, 2), (6, 2), (7, 2), (10, 0), (1, 3), (6, 3), (7, 3), (10, 1), (1, 0), (6, 0), (7, 0), (10, 2), (1, 1), (6, 1), (7, 1), (10, 3),)
PAIRS = (
   (1, 0, 0),
   (6, 0, 0),
   (7, 0, 0),
   (7, 10, 1),
   (1, 6, 0),
   (6, 10, 0),
   (1, 7, 0),
   (6, 7, 0),
   (1, 10, 0),
   (3, 10, 0),
   (11, 7, 0),
   (11, 6, 0),
   (3, 7, 0),
   (11, 1, 0),
   (3, 6, 0),
   (3, 11, 0),
   (9, 3, 0),
   (9, 6, 0),
   (9, 1, 1),
   (2, 11, 0),
   (4, 3, 0),
   (2, 0, 0),
   (4, 0, 1),
   (2, 7, 0),
   (2, 6, 1),
   (4, 11, 0),
   (4, 9, 0),
   (4, 7, 0),
   (8, 4, 1),
   (8, 6, 0),
   (8, 3, 0),
   (5, 8, 1),
   (5, 7, 0),
   (5, 11, 0),
   (5, 4, 1),
)
ARRIVALS = (
    ((1, 2), (6, 2), (7, 2), (10, 0), (1, 3), (6, 3), (7, 3), (10, 1), (3, 2), (11, 0), (1, 0), (6, 0), (7, 0), (10, 2), (3, 3), (11, 1), (1, 1), (6, 1), (7, 1), (10, 3),),
    (),
    (),
    ((3, 0), (11, 2), (2, 2), (4, 2), (8, 3), (9, 0),),
    ((3, 1), (11, 3),),
    ((2, 3), (4, 3), (8, 0), (9, 1),),
    (),
    (),
    ((5, 2), (9, 3), (2, 0), (4, 0), (8, 1), (9, 2),),
    ((5, 3), (2, 1), (4, 1),),
    (),
    (),
    ((5, 0),),
    ((8, 2),),
    (),
    ((5, 1),),
    (),
    (),
)
COUNT = len(TILES)
PIECE = ROWS // CHUNKS


def minus(a, b):
    return tuple((p - q) % 4 for p, q in zip(a, b))


def parent(tile, chunk):
    return TILES.index(minus(TILES[tile], DIRECTIONS[ROUTES[tile][chunk]]))


def children():
    table = {}
    for tile in range(1, COUNT):
        for chunk in range(CHUNKS):
            table.setdefault((parent(tile, chunk), chunk), []).append((tile, chunk))
    return table


CHILDREN = children()
ROW_TILES = sorted({x for x, _, _ in PAIRS})
SHARED_TILES = sorted({y for _, y, _ in PAIRS} | {0})
COL_TILES = sorted({y for _, y, one in PAIRS if not one})


def kept_rows():
    kept = []
    fill = [2] * COUNT
    for number, (x, y, one) in enumerate(PAIRS):
        apart = minus(TILES[y], TILES[x])
        if apart[1] == 0 and apart[0] % 2 == 0:
            back = minus(TILES[x], TILES[y])
            left = (x, fill[x], apart[2] * 2 + apart[0] // 2)
            fill[x] += 1
            right = None
            if not one:
                right = (y, fill[y], back[2] * 2 + back[0] // 2)
                fill[y] += 1
            kept.append((number, left, right))
    return kept


KEPT = kept_rows()
KEPT_OF = {number: place for place, (number, _, _) in enumerate(KEPT)}
SPARE_ROW = COUNT
SPARE_KEPT = len(KEPT)
SPARE_COL = COUNT
KEPT_COL = COUNT + 1


def slots(number):
    x, y, one = PAIRS[number]
    kept = KEPT_OF.get(number, SPARE_KEPT)
    if one:
        col = SPARE_COL
    elif kept != SPARE_KEPT:
        col = KEPT_COL + kept
    else:
        col = y
    return (x, y, x, kept, col)


NOTHING = (0, 0, SPARE_ROW, SPARE_KEPT, SPARE_COL)
ROUNDS = (len(PAIRS) + 1) // 2


def first_use(tile):
    for number, (_, y, _) in enumerate(PAIRS):
        if y == tile:
            return number // 2
    return None


SAME_CORE = {tile: place for place, tile in enumerate(range(1, COUNT))}
CROSS_CORE = {tile: len(SAME_CORE) + place for place, tile in enumerate(COL_TILES)}
MESSAGES = len(SAME_CORE) + len(CROSS_CORE)
SAME_CORE[0] = MESSAGES


def done_round(tile):
    last = max([n for n, (x, y, one) in enumerate(PAIRS) if x == tile or (y == tile and not one)], default=0)
    return min(last // 2 + (2 if last % 2 else 1), ROUNDS)


def kernel(
    cand_ref, embed_ref, counts_ref, tops_ref, recount_ref,
    tiles, near, far, row_sums, row_tops, kept_sums, col_sums, col_tops,
    outbox, inbox, table,
    own_sem, hop_send, hop_recv, twin_send, twin_recv, post_send, post_recv,
):
    my_row = lax.axis_index("row")
    my_col = lax.axis_index("col")
    z, x_hi = lax.div(my_row, 2), lax.rem(my_row, 2)
    y, x_lo, core = lax.div(my_col, 4), lax.rem(lax.div(my_col, 2), 2), lax.rem(my_col, 2)
    x = x_hi * 2 + x_lo
    other = 1 - core
    chips = {}
    for offset in TILES + DIRECTIONS:
        if offset not in chips:
            px = lax.rem(x + offset[0], 4)
            py = lax.rem(y + offset[1], 4)
            pz = lax.rem(z + offset[2], 4)
            chips[offset] = (pz * 2 + lax.div(px, 2), py * 4 + lax.rem(px, 2) * 2)

    def device(offset, at_core):
        row, col = chips[offset]
        return (row, col + at_core)

    def span(chunk):
        return pl.ds(chunk * PIECE, PIECE)

    def hop(tile, chunk):
        origin = parent(tile, chunk)
        step = DIRECTIONS[ROUTES[tile][chunk]]
        source = embed_ref.at[span(chunk)] if origin == 0 else tiles.at[origin, core, span(chunk)]
        return pltpu.make_async_remote_copy(
            src_ref=source,
            dst_ref=tiles.at[tile, core, span(chunk)],
            send_sem=hop_send,
            recv_sem=hop_recv.at[tile, chunk],
            device_id=device(minus((0, 0, 0), step), core),
            device_id_type=MESH,
        )

    def twin(tile, chunk):
        source = embed_ref.at[span(chunk)] if tile == 0 else tiles.at[tile, core, span(chunk)]
        return pltpu.make_async_remote_copy(
            src_ref=source,
            dst_ref=tiles.at[tile, core, span(chunk)],
            send_sem=twin_send,
            recv_sem=twin_recv.at[tile],
            device_id=device((0, 0, 0), other),
            device_id_type=MESH,
        )

    def twin_whole(tile):
        return pltpu.make_async_remote_copy(
            src_ref=tiles.at[tile, other],
            dst_ref=tiles.at[tile, other],
            send_sem=twin_send,
            recv_sem=twin_recv.at[tile],
            device_id=device((0, 0, 0), other),
            device_id_type=MESH,
        )

    def post(tile, place, at_core):
        return pltpu.make_async_remote_copy(
            src_ref=outbox.at[place],
            dst_ref=inbox.at[place],
            send_sem=post_send,
            recv_sem=post_recv,
            device_id=device(TILES[tile], at_core),
            device_id_type=MESH,
        )

    own = pltpu.make_async_copy(embed_ref, tiles.at[0, core], own_sem)
    own.start()

    barrier = pltpu.get_barrier_semaphore()
    for step in DIRECTIONS:
        pl.semaphore_signal(barrier, inc=1, device_id=device(step, core), device_id_type=MESH)
    pl.semaphore_signal(barrier, inc=1, device_id=device((0, 0, 0), other), device_id_type=MESH)
    pl.semaphore_wait(barrier, 7)

    for tile, chunk in FIRST:
        hop(tile, chunk).start()
    for chunk in range(CHUNKS):
        twin(0, chunk).start()

    row_sums[...] = jnp.zeros_like(row_sums)
    col_sums[...] = jnp.zeros_like(col_sums)
    row_tops[...] = jnp.full_like(row_tops, LOWEST)
    col_tops[...] = jnp.full_like(col_tops, LOWEST)
    far[...] = jnp.zeros_like(far)

    def multiply(target, left, right):
        target[...] = lax.dot_general(
            tiles[left, core], tiles[right].reshape(2 * ROWS, WIDTH), TRANSPOSED,
            preferred_element_type=jnp.float32,
        )

    def halves(op, values):
        return (
            op(values[:, 0:128], values[:, 128:256]),
            op(values[:, 256:384], values[:, 384:512]),
        )

    def reduce(source, row, kept, col, own_pair=False):
        sums = tops = None
        for first in range(0, ROWS, 64):
            part = pl.ds(first, 64)
            scores = source[part, :]
            weights = jnp.exp2(scores * SCALE - SCALE)
            if own_pair:
                place = lax.broadcasted_iota(jnp.int32, (64, 2 * ROWS), 0) + (first + core * ROWS)
                itself = place == lax.broadcasted_iota(jnp.int32, (64, 2 * ROWS), 1)
                weights = jnp.where(itself, 0.0, weights)
                scores = jnp.where(itself, LOWEST, scores)
            left, right = halves(jnp.add, weights)
            row_sums[row, part] += left + right
            kept_sums[kept, part] = jnp.where(core == 0, left, right)
            row_tops[row, part] = jnp.maximum(
                row_tops[row, part], jnp.maximum(*halves(jnp.maximum, scores))
            )
            if own_pair:
                continue
            for at in range(0, 64, 8):
                sums = weights[at:at + 8] if sums is None else sums + weights[at:at + 8]
                high = scores[at:at + 8]
                tops = high if tops is None else jnp.maximum(tops, high)
        if not own_pair:
            col_sums[col] += sums
            col_tops[col] = jnp.maximum(col_tops[col], tops)

    def arrive(tile, chunk):
        hop(tile, chunk).wait_recv()
        for child, piece in CHILDREN.get((tile, chunk), ()):
            hop(child, piece).start()
        if tile in SHARED_TILES:
            twin(tile, chunk).start()

    own.wait()
    twin_whole(0).wait_recv()
    multiply(near, 0, 0)
    reduce(near, 0, SPARE_KEPT + 1, SPARE_COL, own_pair=True)

    def across(values, op):
        return op(values.T, axis=0, keepdims=True)

    def column(values, op, half):
        mine = jnp.where(core == half, values[:, :ROWS], values[:, ROWS:])
        return op(mine, axis=0, keepdims=True)

    def finish(tile):
        places = {0: SAME_CORE[tile]}
        if tile in COL_TILES:
            places[1] = CROSS_CORE[tile]
        for half, place in reversed(places.items()):
            sums = tops = None
            if tile in COL_TILES:
                sums = column(col_sums[tile], jnp.sum, half)
                tops = column(col_tops[tile], jnp.max, half)
            for at, (_, _, right) in enumerate(KEPT):
                if right is not None and right[0] == tile:
                    extra = column(col_sums[KEPT_COL + at], jnp.sum, half)
                    sums = sums + extra
                    tops = jnp.maximum(tops, column(col_tops[KEPT_COL + at], jnp.max, half))
                    if half == 0:
                        outbox[place, pl.ds(right[1], 1), :] = extra
            if half == 0 and (tile in ROW_TILES or tile == 0):
                low, high = across(row_sums[tile], jnp.sum), across(row_tops[tile], jnp.max)
                sums = low if sums is None else sums + low
                tops = high if tops is None else jnp.maximum(tops, high)
                for at, (_, left, _) in enumerate(KEPT):
                    if left[0] == tile:
                        outbox[place, pl.ds(left[1], 1), :] = across(kept_sums[at], jnp.sum)
            outbox[place, 0:1, :] = sums
            outbox[place, 1:2, :] = tops
            if place != MESSAGES:
                post(tile, place, other if half else core).start()

    def arrivals(number):
        def run():
            for tile, chunk in ARRIVALS[number]:
                arrive(tile, chunk)
            for tile in SHARED_TILES:
                if tile != 0 and first_use(tile) == number:
                    twin_whole(tile).wait_recv()
            for tile in range(COUNT):
                if done_round(tile) == number:
                    finish(tile)
            values = []
            for step in (2 * number, 2 * number + 1):
                values += slots(step) if step < len(PAIRS) else NOTHING
            return tuple(jnp.int32(v) for v in values)
        return run

    def round_of(number, before):
        now = lax.switch(number, [arrivals(n) for n in range(ROUNDS)])
        multiply(near, now[0], now[1])
        reduce(far, *before)
        multiply(far, now[5], now[6])
        reduce(near, *now[2:5])
        return tuple(now[7:10])

    last = lax.fori_loop(
        0, ROUNDS, round_of, tuple(jnp.int32(v) for v in NOTHING[2:5])
    )
    reduce(far, *last)
    for tile in list(range(1, COUNT)) + [0]:
        if done_round(tile) == ROUNDS:
            finish(tile)
    table[0:1, :] = across(kept_sums[SPARE_KEPT + 1], jnp.sum)

    moved = tiles.at[pl.ds(1, COUNT - 1), core]
    pltpu.make_async_copy(moved, moved, hop_send).wait()
    shared = tiles.at[pl.ds(0, len(SHARED_TILES)), core]
    pltpu.make_async_copy(shared, shared, twin_send).wait()
    sent = outbox.at[pl.ds(0, MESSAGES)]
    pltpu.make_async_copy(sent, sent, post_send).wait()
    pltpu.make_async_copy(inbox, inbox, post_recv).wait()

    sums = tops = outbox[MESSAGES]
    for place in range(MESSAGES):
        sums = sums + inbox[place]
        tops = jnp.maximum(tops, inbox[place])
    counts_ref[...] = sums[0:1, :]
    tops_ref[...] = tops[1:2, :]
    for _, left, right in KEPT:
        for side in (left, right):
            if side is not None:
                where = outbox if side[0] == 0 else inbox
                table[pl.ds(side[2], 1), :] = where[SAME_CORE[side[0]], pl.ds(side[1], 1), :]
    for number in range(2):
        chosen = cand_ref[number]
        apart = ((chosen // 2 - z + 4) % 4) * 2 + (chosen % 2 - x_hi + 2) % 2
        recount_ref[pl.ds(number, 1), :] = table[pl.ds(apart, 1), :]


def per_device(embed, cand_tiles):
    vector = pltpu.VMEM
    semaphores = pltpu.SemaphoreType.DMA
    counts, tops, recount = pl.pallas_call(
        kernel,
        out_shape=(
            jax.ShapeDtypeStruct((1, ROWS), jnp.float32),
            jax.ShapeDtypeStruct((1, ROWS), jnp.float32),
            jax.ShapeDtypeStruct((2, ROWS), jnp.float32),
        ),
        in_specs=[
            pl.BlockSpec(memory_space=pltpu.SMEM),
            pl.BlockSpec(memory_space=pl.ANY),
        ],
        out_specs=[pl.BlockSpec(memory_space=pltpu.VMEM)] * 3,
        scratch_shapes=[
            vector((COUNT, 2, ROWS, WIDTH), jnp.bfloat16),
            vector((ROWS, 2 * ROWS), jnp.float32),
            vector((ROWS, 2 * ROWS), jnp.float32),
            vector((COUNT + 1, ROWS, 128), jnp.float32),
            vector((COUNT + 1, ROWS, 128), jnp.float32),
            vector((SPARE_KEPT + 2, ROWS, 128), jnp.float32),
            vector((KEPT_COL + len(KEPT), 8, 2 * ROWS), jnp.float32),
            vector((KEPT_COL + len(KEPT), 8, 2 * ROWS), jnp.float32),
            vector((MESSAGES + 1, 8, ROWS), jnp.float32),
            vector((MESSAGES, 8, ROWS), jnp.float32),
            vector((8, ROWS), jnp.float32),
            semaphores,
            semaphores,
            semaphores((COUNT, CHUNKS)),
            semaphores,
            semaphores((COUNT,)),
            semaphores,
            semaphores,
        ],
        compiler_params=pltpu.CompilerParams(
            collective_id=0, has_side_effects=True, vmem_limit_bytes=56 * 1024 * 1024
        ),
        cost_estimate=pl.CostEstimate(
            flops=37 * 2 * ROWS * 2 * ROWS * WIDTH,
            bytes_accessed=COUNT * 2 * ROWS * WIDTH * 2,
            transcendentals=37 * ROWS * 2 * ROWS,
        ),
    )(cand_tiles, embed)
    return counts.reshape(ROWS), tops.reshape(ROWS), recount


def solution(mesh):
    in_specs = (P(("row", "col"), None), P(("row", "col")))
    out_specs = (P(("row", "col")), P(("row", "col")), P(("row", "col"), None))
    return jax.shard_map(
        per_device, mesh=mesh, in_specs=in_specs, out_specs=out_specs, check_vma=False
    )
```

```python
import jax
import jax.numpy as jnp
from jax import lax
from jax.experimental import pallas as pl
from jax.experimental.pallas import tpu as pltpu
from jax.sharding import PartitionSpec as P

MESH = pl.DeviceIdType.MESH
ROWS = 256
WIDTH = 768
SCALE = 20.0 * 1.4426950408889634
LOWEST = -3.0
TRANSPOSED = (((1,), (1,)), ((), ()))
DIRECTIONS = ((1, 0, 0), (3, 0, 0), (0, 1, 0), (0, 3, 0), (0, 0, 1), (0, 0, 3))
CHUNKS = 4
TILES = (
   (0, 0, 0),
   (0, 0, 1),
   (0, 1, 0),
   (0, 1, 3),
   (0, 2, 0),
   (0, 2, 3),
   (0, 3, 0),
   (1, 0, 0),
   (2, 0, 0),
   (2, 0, 2),
   (3, 0, 1),
   (3, 0, 2),
)
ROUTES = (
    (),
   (4, 4, 4, 4),
   (2, 2, 2, 2),
   (5, 5, 5, 5),
   (3, 3, 4, 3),
   (2, 2, 2, 5),
   (3, 3, 3, 3),
   (0, 0, 0, 0),
   (0, 0, 0, 0),
   (1, 1, 1, 1),
   (1, 1, 1, 1),
   (4, 4, 4, 4),
)
FIRST = ((1, 2), (2, 0), (6, 2), (7, 0), (1, 3), (2, 1), (6, 3), (7, 1), (1, 0), (2, 2), (6, 0), (7, 2), (1, 1), (2, 3), (6, 1), (7, 3),)
PAIRS = (
   (1, 0, 0),
   (2, 0, 0),
   (7, 0, 0),
   (1, 6, 0),
   (1, 2, 0),
   (2, 6, 1),
   (2, 7, 0),
   (6, 7, 0),
   (1, 7, 0),
   (10, 2, 0),
   (10, 7, 0),
   (10, 6, 0),
   (3, 7, 0),
   (3, 1, 0),
   (3, 6, 0),
   (3, 10, 0),
   (5, 7, 0),
   (5, 10, 0),
   (5, 1, 1),
   (8, 3, 0),
   (11, 0, 0),
   (8, 5, 0),
   (8, 2, 0),
   (11, 7, 1),
   (8, 0, 1),
   (11, 6, 0),
   (8, 10, 0),
   (11, 3, 0),
   (4, 10, 0),
   (4, 7, 0),
   (4, 8, 1),
   (9, 4, 1),
   (9, 2, 0),
   (9, 3, 0),
   (9, 8, 1),
)
ARRIVALS = (
    ((1, 2), (2, 0), (6, 2), (7, 0), (1, 3), (2, 1), (6, 3), (7, 1), (3, 0), (10, 2), (1, 0), (2, 2), (6, 0), (7, 2), (3, 1), (10, 3), (1, 1), (2, 3), (6, 1), (7, 3),),
    (),
    (),
    (),
    (),
    ((3, 2), (10, 0), (4, 3), (5, 0), (8, 0), (11, 2),),
    (),
    (),
    (),
    ((3, 3), (10, 1), (4, 0), (5, 1), (8, 1), (11, 3),),
    (),
    (),
    (),
    (),
    (),
    ((5, 3), (9, 2), (4, 1), (5, 2), (8, 2), (11, 0),),
    (),
    (),
    (),
    ((9, 3), (8, 3), (11, 1),),
    (),
    (),
    (),
    (),
    ((9, 0),),
    ((4, 2),),
    (),
    (),
    (),
    (),
    (),
    ((9, 1),),
    (),
    (),
    (),
)
COUNT = len(TILES)
PIECE = ROWS // CHUNKS


def minus(a, b):
    return tuple((p - q) % 4 for p, q in zip(a, b))


def parent(tile, chunk):
    return TILES.index(minus(TILES[tile], DIRECTIONS[ROUTES[tile][chunk]]))


def children():
    table = {}
    for tile in range(1, COUNT):
        for chunk in range(CHUNKS):
            table.setdefault((parent(tile, chunk), chunk), []).append((tile, chunk))
    return table


CHILDREN = children()
ROW_TILES = sorted({x for x, _, _ in PAIRS})
SHARED_TILES = sorted({y for _, y, _ in PAIRS} | {0})
COL_TILES = sorted({y for _, y, one in PAIRS if not one})


def kept_rows():
    kept = []
    fill = [2] * COUNT
    for number, (x, y, one) in enumerate(PAIRS):
        apart = minus(TILES[y], TILES[x])
        if apart[1] == 0 and apart[0] % 2 == 0:
            back = minus(TILES[x], TILES[y])
            left = (x, fill[x], apart[2] * 2 + apart[0] // 2)
            fill[x] += 1
            right = None
            if not one:
                right = (y, fill[y], back[2] * 2 + back[0] // 2)
                fill[y] += 1
            kept.append((number, left, right))
    return kept


KEPT = kept_rows()
KEPT_OF = {number: place for place, (number, _, _) in enumerate(KEPT)}
SPARE_ROW = COUNT
SPARE_KEPT = len(KEPT)
SPARE_COL = COUNT
KEPT_COL = COUNT + 1


def slots(number):
    x, y, one = PAIRS[number]
    kept = KEPT_OF.get(number, SPARE_KEPT)
    if one:
        col = SPARE_COL
    elif kept != SPARE_KEPT:
        col = KEPT_COL + kept
    else:
        col = y
    return (x, y, x, kept, col)


NOTHING = (0, 0, SPARE_ROW, SPARE_KEPT, SPARE_COL)
ROUNDS = (len(PAIRS) + 1) // 2


def first_use(tile):
    for number, (_, y, _) in enumerate(PAIRS):
        if y == tile:
            return number
    return None


SAME_CORE = {tile: place for place, tile in enumerate(range(1, COUNT))}
CROSS_CORE = {tile: len(SAME_CORE) + place for place, tile in enumerate(COL_TILES)}
MESSAGES = len(SAME_CORE) + len(CROSS_CORE)
SAME_CORE[0] = MESSAGES


def last_round(tile, cols):
    steps = [n for n, (x, y, one) in enumerate(PAIRS) if x == tile or (cols and y == tile and not one)]
    last = max(steps, default=-1)
    return 0 if last < 0 else last // 2 + last % 2


def lane_rounds():
    rows, kept, free = {}, {}, {}
    for tile in sorted(ROW_TILES + ([] if 0 in ROW_TILES else [0]), key=lambda t: last_round(t, False)):
        at = last_round(tile, False) + 1
        while at in free:
            at += 1
        free[at] = tile
        rows[tile] = at
    used = set()
    for place, (number, _, _) in enumerate(KEPT):
        at = number // 2 + number % 2 + 1
        while at in used:
            at += 1
        used.add(at)
        kept[place] = at
    return rows, kept


LANE_ROWS, LANE_KEPT = lane_rounds()


def done_round(tile):
    at = last_round(tile, True) + 1
    if LANE_ROWS.get(tile, -1) < ROUNDS:
        at = max(at, LANE_ROWS.get(tile, -1) + 1)
    for place, (_, left, _) in enumerate(KEPT):
        if left[0] == tile and LANE_KEPT[place] < ROUNDS:
            at = max(at, LANE_KEPT[place] + 1)
    if LANE_ROWS.get(tile, -1) >= ROUNDS:
        at = ROUNDS
    for place, (_, left, _) in enumerate(KEPT):
        if left[0] == tile and LANE_KEPT[place] >= ROUNDS:
            at = ROUNDS
    return min(at, ROUNDS)


def kernel(
    cand_ref, embed_ref, counts_ref, tops_ref, recount_ref,
    tiles, near, far, row_sums, row_tops, kept_sums, col_sums, col_tops,
    row_lanes, kept_lanes, outbox, inbox, table,
    own_sem, hop_send, hop_recv, twin_send, twin_recv, post_send, post_recv,
):
    my_row = lax.axis_index("row")
    my_col = lax.axis_index("col")
    z, x_hi = lax.div(my_row, 2), lax.rem(my_row, 2)
    y, x_lo, core = lax.div(my_col, 4), lax.rem(lax.div(my_col, 2), 2), lax.rem(my_col, 2)
    x = x_hi * 2 + x_lo
    other = 1 - core
    chips = {}
    for offset in TILES + DIRECTIONS:
        if offset not in chips:
            px = lax.rem(x + offset[0], 4)
            py = lax.rem(y + offset[1], 4)
            pz = lax.rem(z + offset[2], 4)
            chips[offset] = (pz * 2 + lax.div(px, 2), py * 4 + lax.rem(px, 2) * 2)

    def device(offset, at_core):
        row, col = chips[offset]
        return (row, col + at_core)

    def span(chunk):
        return pl.ds(chunk * PIECE, PIECE)

    def hop(tile, chunk):
        origin = parent(tile, chunk)
        step = DIRECTIONS[ROUTES[tile][chunk]]
        source = embed_ref.at[span(chunk)] if origin == 0 else tiles.at[origin, core, span(chunk)]
        return pltpu.make_async_remote_copy(
            src_ref=source,
            dst_ref=tiles.at[tile, core, span(chunk)],
            send_sem=hop_send,
            recv_sem=hop_recv.at[tile, chunk],
            device_id=device(minus((0, 0, 0), step), core),
            device_id_type=MESH,
        )

    def twin(tile, chunk):
        source = embed_ref.at[span(chunk)] if tile == 0 else tiles.at[tile, core, span(chunk)]
        return pltpu.make_async_remote_copy(
            src_ref=source,
            dst_ref=tiles.at[tile, core, span(chunk)],
            send_sem=twin_send,
            recv_sem=twin_recv.at[tile],
            device_id=device((0, 0, 0), other),
            device_id_type=MESH,
        )

    def twin_whole(tile):
        return pltpu.make_async_remote_copy(
            src_ref=tiles.at[tile, other],
            dst_ref=tiles.at[tile, other],
            send_sem=twin_send,
            recv_sem=twin_recv.at[tile],
            device_id=device((0, 0, 0), other),
            device_id_type=MESH,
        )

    def post(tile, place, at_core):
        return pltpu.make_async_remote_copy(
            src_ref=outbox.at[place],
            dst_ref=inbox.at[place],
            send_sem=post_send,
            recv_sem=post_recv,
            device_id=device(TILES[tile], at_core),
            device_id_type=MESH,
        )

    own = pltpu.make_async_copy(embed_ref, tiles.at[0, core], own_sem)
    own.start()

    barrier = pltpu.get_barrier_semaphore()
    for step in DIRECTIONS:
        pl.semaphore_signal(barrier, inc=1, device_id=device(step, core), device_id_type=MESH)
    pl.semaphore_signal(barrier, inc=1, device_id=device((0, 0, 0), other), device_id_type=MESH)
    pl.semaphore_wait(barrier, 7)

    for tile, chunk in FIRST:
        hop(tile, chunk).start()
    for chunk in range(CHUNKS):
        twin(0, chunk).start()

    row_sums[...] = jnp.zeros_like(row_sums)
    col_sums[...] = jnp.zeros_like(col_sums)
    row_tops[...] = jnp.full_like(row_tops, LOWEST)
    col_tops[...] = jnp.full_like(col_tops, LOWEST)
    far[...] = jnp.zeros_like(far)

    def multiply(target, left, right):
        target[...] = lax.dot_general(
            tiles[left, core], tiles[right].reshape(2 * ROWS, WIDTH), TRANSPOSED,
            preferred_element_type=jnp.float32,
        )

    def halves(op, values):
        return (
            op(values[:, 0:128], values[:, 128:256]),
            op(values[:, 256:384], values[:, 384:512]),
        )

    def reduce(source, row, kept, col, own_pair=False):
        sums = tops = None
        for first in range(0, ROWS, 64):
            part = pl.ds(first, 64)
            scores = source[part, :]
            weights = jnp.exp2(scores * SCALE - SCALE)
            if own_pair:
                place = lax.broadcasted_iota(jnp.int32, (64, 2 * ROWS), 0) + (first + core * ROWS)
                itself = place == lax.broadcasted_iota(jnp.int32, (64, 2 * ROWS), 1)
                weights = jnp.where(itself, 0.0, weights)
                scores = jnp.where(itself, LOWEST, scores)
            left, right = halves(jnp.add, weights)
            row_sums[row, part] += left + right
            kept_sums[kept, part] = jnp.where(core == 0, left, right)
            row_tops[row, part] = jnp.maximum(
                row_tops[row, part], jnp.maximum(*halves(jnp.maximum, scores))
            )
            if own_pair:
                continue
            for at in range(0, 64, 8):
                sums = weights[at:at + 8] if sums is None else sums + weights[at:at + 8]
                high = scores[at:at + 8]
                tops = high if tops is None else jnp.maximum(tops, high)
        if not own_pair:
            col_sums[col] += sums
            col_tops[col] = jnp.maximum(col_tops[col], tops)

    def arrive(tile, chunk):
        hop(tile, chunk).wait_recv()
        for child, piece in CHILDREN.get((tile, chunk), ()):
            hop(child, piece).start()
        if tile in SHARED_TILES:
            twin(tile, chunk).start()

    own.wait()
    twin_whole(0).wait_recv()
    multiply(near, 0, 0)
    reduce(near, 0, SPARE_KEPT + 1, SPARE_COL, own_pair=True)

    def across(values, op):
        return op(values.T, axis=0, keepdims=True)

    def column(values, op, half):
        mine = jnp.where(core == half, values[:, :ROWS], values[:, ROWS:])
        return op(mine, axis=0, keepdims=True)

    def finish(tile):
        places = {0: SAME_CORE[tile]}
        if tile in COL_TILES:
            places[1] = CROSS_CORE[tile]
        for half, place in reversed(places.items()):
            sums = tops = None
            if tile in COL_TILES:
                sums = column(col_sums[tile], jnp.sum, half)
                tops = column(col_tops[tile], jnp.max, half)
            for at, (_, _, right) in enumerate(KEPT):
                if right is not None and right[0] == tile:
                    extra = column(col_sums[KEPT_COL + at], jnp.sum, half)
                    sums = sums + extra
                    tops = jnp.maximum(tops, column(col_tops[KEPT_COL + at], jnp.max, half))
                    if half == 0:
                        outbox[place, pl.ds(right[1], 1), :] = extra
            if half == 0 and (tile in ROW_TILES or tile == 0):
                if LANE_ROWS[tile] < ROUNDS:
                    low, high = row_lanes[tile, 0:1, :], row_lanes[tile, 1:2, :]
                else:
                    low, high = across(row_sums[tile], jnp.sum), across(row_tops[tile], jnp.max)
                sums = low if sums is None else sums + low
                tops = high if tops is None else jnp.maximum(tops, high)
                for at, (_, left, _) in enumerate(KEPT):
                    if left[0] == tile:
                        if LANE_KEPT[at] < ROUNDS:
                            kept = kept_lanes[at, 0:1, :]
                        else:
                            kept = across(kept_sums[at], jnp.sum)
                        outbox[place, pl.ds(left[1], 1), :] = kept
            outbox[place, 0:1, :] = sums
            outbox[place, 1:2, :] = tops
            if place != MESSAGES:
                post(tile, place, other if half else core).start()

    def lanes(row, kept):
        row_lanes[row, 0:1, :] = across(row_sums[row], jnp.sum)
        row_lanes[row, 1:2, :] = across(row_tops[row], jnp.max)
        kept_lanes[kept, 0:1, :] = across(kept_sums[kept], jnp.sum)

    def arrivals(number, second):
        if True:
            step = 2 * number + second
            if step < len(PAIRS):
                for tile, chunk in ARRIVALS[step]:
                    arrive(tile, chunk)
                for tile in SHARED_TILES:
                    if tile != 0 and first_use(tile) == step:
                        twin_whole(tile).wait_recv()
            values = slots(step) if step < len(PAIRS) else NOTHING
            if not second:
                row = [tile for tile, at in LANE_ROWS.items() if at == number] or [SPARE_ROW]
                kept = [place for place, at in LANE_KEPT.items() if at == number] or [SPARE_KEPT]
                values = values + (row[0], kept[0])
                for tile in range(COUNT):
                    if done_round(tile) == number:
                        finish(tile)
            return values

    before = NOTHING[2:5]
    for number in range(ROUNDS):
        one, two = arrivals(number, 0), arrivals(number, 1)
        lanes(*one[5:7])
        multiply(near, one[0], one[1])
        reduce(far, *before)
        multiply(far, two[0], two[1])
        reduce(near, *one[2:5])
        before = two[2:5]
    last = before
    reduce(far, *last)
    for tile in list(range(1, COUNT)) + [0]:
        if done_round(tile) == ROUNDS:
            finish(tile)
    table[0:1, :] = across(kept_sums[SPARE_KEPT + 1], jnp.sum)

    moved = tiles.at[pl.ds(1, COUNT - 1), core]
    pltpu.make_async_copy(moved, moved, hop_send).wait()
    shared = tiles.at[pl.ds(0, len(SHARED_TILES)), core]
    pltpu.make_async_copy(shared, shared, twin_send).wait()
    sent = outbox.at[pl.ds(0, MESSAGES)]
    pltpu.make_async_copy(sent, sent, post_send).wait()
    pltpu.make_async_copy(inbox, inbox, post_recv).wait()

    sums = tops = outbox[MESSAGES]
    for place in range(MESSAGES):
        sums = sums + inbox[place]
        tops = jnp.maximum(tops, inbox[place])
    counts_ref[...] = sums[0:1, :]
    tops_ref[...] = tops[1:2, :]
    for _, left, right in KEPT:
        for side in (left, right):
            if side is not None:
                where = outbox if side[0] == 0 else inbox
                table[pl.ds(side[2], 1), :] = where[SAME_CORE[side[0]], pl.ds(side[1], 1), :]
    for number in range(2):
        chosen = cand_ref[number]
        apart = ((chosen // 2 - z + 4) % 4) * 2 + (chosen % 2 - x_hi + 2) % 2
        recount_ref[pl.ds(number, 1), :] = table[pl.ds(apart, 1), :]


def per_device(embed, cand_tiles):
    vector = pltpu.VMEM
    semaphores = pltpu.SemaphoreType.DMA
    counts, tops, recount = pl.pallas_call(
        kernel,
        out_shape=(
            jax.ShapeDtypeStruct((1, ROWS), jnp.float32),
            jax.ShapeDtypeStruct((1, ROWS), jnp.float32),
            jax.ShapeDtypeStruct((2, ROWS), jnp.float32),
        ),
        in_specs=[
            pl.BlockSpec(memory_space=pltpu.SMEM),
            pl.BlockSpec(memory_space=pl.ANY),
        ],
        out_specs=[pl.BlockSpec(memory_space=pltpu.VMEM)] * 3,
        scratch_shapes=[
            vector((COUNT, 2, ROWS, WIDTH), jnp.bfloat16),
            vector((ROWS, 2 * ROWS), jnp.float32),
            vector((ROWS, 2 * ROWS), jnp.float32),
            vector((COUNT + 1, ROWS, 128), jnp.float32),
            vector((COUNT + 1, ROWS, 128), jnp.float32),
            vector((SPARE_KEPT + 2, ROWS, 128), jnp.float32),
            vector((KEPT_COL + len(KEPT), 8, 2 * ROWS), jnp.float32),
            vector((KEPT_COL + len(KEPT), 8, 2 * ROWS), jnp.float32),
            vector((COUNT + 1, 8, ROWS), jnp.float32),
            vector((SPARE_KEPT + 1, 8, ROWS), jnp.float32),
            vector((MESSAGES + 1, 8, ROWS), jnp.float32),
            vector((MESSAGES, 8, ROWS), jnp.float32),
            vector((8, ROWS), jnp.float32),
            semaphores,
            semaphores,
            semaphores((COUNT, CHUNKS)),
            semaphores,
            semaphores((COUNT,)),
            semaphores,
            semaphores,
        ],
        compiler_params=pltpu.CompilerParams(
            collective_id=0, has_side_effects=True, vmem_limit_bytes=56 * 1024 * 1024
        ),
        cost_estimate=pl.CostEstimate(
            flops=37 * 2 * ROWS * 2 * ROWS * WIDTH,
            bytes_accessed=COUNT * 2 * ROWS * WIDTH * 2,
            transcendentals=37 * ROWS * 2 * ROWS,
        ),
    )(cand_tiles, embed)
    return counts.reshape(ROWS), tops.reshape(ROWS), recount


def solution(mesh):
    in_specs = (P(("row", "col"), None), P(("row", "col")))
    out_specs = (P(("row", "col")), P(("row", "col")), P(("row", "col"), None))
    return jax.shard_map(
        per_device, mesh=mesh, in_specs=in_specs, out_specs=out_specs, check_vma=False
    )
```

```python
import jax
import jax.numpy as jnp
from jax import lax
from jax.experimental import pallas as pl
from jax.experimental.pallas import tpu as pltpu
from jax.sharding import PartitionSpec as P

MESH = pl.DeviceIdType.MESH
ROWS = 256
WIDTH = 768
SCALE = 20.0 * 1.4426950408889634
LOWEST = -3.0
TRANSPOSED = (((1,), (1,)), ((), ()))
DIRECTIONS = ((1, 0, 0), (3, 0, 0), (0, 1, 0), (0, 3, 0), (0, 0, 1), (0, 0, 3))
CHUNKS = 4
TILES = (
   (0, 0, 0),
   (0, 0, 1),
   (0, 1, 0),
   (0, 1, 3),
   (0, 2, 0),
   (0, 2, 3),
   (0, 3, 0),
   (1, 0, 0),
   (2, 0, 0),
   (2, 0, 2),
   (3, 0, 1),
   (3, 0, 2),
)
ROUTES = (
    (),
   (4, 4, 4, 4),
   (2, 2, 2, 2),
   (5, 5, 5, 5),
   (3, 3, 4, 3),
   (2, 2, 2, 5),
   (3, 3, 3, 3),
   (0, 0, 0, 0),
   (0, 0, 0, 0),
   (1, 1, 1, 1),
   (1, 1, 1, 1),
   (4, 4, 4, 4),
)
FIRST = ((1, 2), (2, 0), (6, 2), (7, 0), (1, 3), (2, 1), (6, 3), (7, 1), (1, 0), (2, 2), (6, 0), (7, 2), (1, 1), (2, 3), (6, 1), (7, 3),)
PAIRS = (
   (1, 0, 0),
   (2, 0, 0),
   (7, 0, 0),
   (1, 6, 0),
   (1, 2, 0),
   (2, 6, 1),
   (2, 7, 0),
   (6, 7, 0),
   (1, 7, 0),
   (10, 2, 0),
   (10, 7, 0),
   (10, 6, 0),
   (3, 7, 0),
   (3, 1, 0),
   (3, 6, 0),
   (3, 10, 0),
   (5, 7, 0),
   (5, 10, 0),
   (5, 1, 1),
   (8, 3, 0),
   (11, 0, 0),
   (8, 5, 0),
   (8, 2, 0),
   (11, 7, 1),
   (8, 0, 1),
   (11, 6, 0),
   (8, 10, 0),
   (11, 3, 0),
   (4, 10, 0),
   (4, 7, 0),
   (4, 8, 1),
   (9, 4, 1),
   (9, 2, 0),
   (9, 3, 0),
   (9, 8, 1),
)
ARRIVALS = (
    ((1, 2), (2, 0), (6, 2), (7, 0), (1, 3), (2, 1), (6, 3), (7, 1), (3, 0), (10, 2), (1, 0), (2, 2), (6, 0), (7, 2), (3, 1), (10, 3), (1, 1), (2, 3), (6, 1), (7, 3),),
    (),
    (),
    (),
    (),
    ((3, 2), (10, 0), (4, 3), (5, 0), (8, 0), (11, 2),),
    (),
    (),
    (),
    ((3, 3), (10, 1), (4, 0), (5, 1), (8, 1), (11, 3),),
    (),
    (),
    (),
    (),
    (),
    ((5, 3), (9, 2), (4, 1), (5, 2), (8, 2), (11, 0),),
    (),
    (),
    (),
    ((9, 3), (8, 3), (11, 1),),
    (),
    (),
    (),
    (),
    ((9, 0),),
    ((4, 2),),
    (),
    (),
    (),
    (),
    (),
    ((9, 1),),
    (),
    (),
    (),
)
COUNT = len(TILES)
PIECE = ROWS // CHUNKS


def minus(a, b):
    return tuple((p - q) % 4 for p, q in zip(a, b))


def parent(tile, chunk):
    return TILES.index(minus(TILES[tile], DIRECTIONS[ROUTES[tile][chunk]]))


def children():
    table = {}
    for tile in range(1, COUNT):
        for chunk in range(CHUNKS):
            table.setdefault((parent(tile, chunk), chunk), []).append((tile, chunk))
    return table


CHILDREN = children()
ROW_TILES = sorted({x for x, _, _ in PAIRS})
SHARED_TILES = sorted({y for _, y, _ in PAIRS} | {0})
COL_TILES = sorted({y for _, y, one in PAIRS if not one})


def kept_rows():
    kept = []
    fill = [2] * COUNT
    for number, (x, y, one) in enumerate(PAIRS):
        apart = minus(TILES[y], TILES[x])
        if apart[1] == 0 and apart[0] % 2 == 0:
            back = minus(TILES[x], TILES[y])
            left = (x, fill[x], apart[2] * 2 + apart[0] // 2)
            fill[x] += 1
            right = None
            if not one:
                right = (y, fill[y], back[2] * 2 + back[0] // 2)
                fill[y] += 1
            kept.append((number, left, right))
    return kept


KEPT = kept_rows()
KEPT_OF = {number: place for place, (number, _, _) in enumerate(KEPT)}
SPARE_ROW = COUNT
SPARE_KEPT = len(KEPT)
SPARE_COL = COUNT
KEPT_COL = COUNT + 1


def slots(number):
    x, y, one = PAIRS[number]
    kept = KEPT_OF.get(number, SPARE_KEPT)
    if one:
        col = SPARE_COL
    elif kept != SPARE_KEPT:
        col = KEPT_COL + kept
    else:
        col = y
    return (x, y, x, kept, col)


NOTHING = (0, 0, SPARE_ROW, SPARE_KEPT, SPARE_COL)
ROUNDS = (len(PAIRS) + 1) // 2


def first_use(tile):
    for number, (_, y, _) in enumerate(PAIRS):
        if y == tile:
            return number
    return None


SAME_CORE = {tile: place for place, tile in enumerate(range(1, COUNT))}
CROSS_CORE = {tile: len(SAME_CORE) + place for place, tile in enumerate(COL_TILES)}
MESSAGES = len(SAME_CORE) + len(CROSS_CORE)
SAME_CORE[0] = MESSAGES


def last_round(tile, cols):
    steps = [n for n, (x, y, one) in enumerate(PAIRS) if x == tile or (cols and y == tile and not one)]
    last = max(steps, default=-1)
    return 0 if last < 0 else last // 2 + last % 2


def lane_rounds():
    rows, kept, free = {}, {}, {}
    for tile in sorted(ROW_TILES + ([] if 0 in ROW_TILES else [0]), key=lambda t: last_round(t, False)):
        at = last_round(tile, False) + 1
        while at in free:
            at += 1
        free[at] = tile
        rows[tile] = at
    used = set()
    for place, (number, _, _) in enumerate(KEPT):
        at = number // 2 + number % 2 + 1
        while at in used:
            at += 1
        used.add(at)
        kept[place] = at
    return rows, kept


LANE_ROWS, LANE_KEPT = lane_rounds()


def done_round(tile):
    at = last_round(tile, True) + 1
    if LANE_ROWS.get(tile, -1) < ROUNDS:
        at = max(at, LANE_ROWS.get(tile, -1) + 1)
    for place, (_, left, _) in enumerate(KEPT):
        if left[0] == tile and LANE_KEPT[place] < ROUNDS:
            at = max(at, LANE_KEPT[place] + 1)
    if LANE_ROWS.get(tile, -1) >= ROUNDS:
        at = ROUNDS
    for place, (_, left, _) in enumerate(KEPT):
        if left[0] == tile and LANE_KEPT[place] >= ROUNDS:
            at = ROUNDS
    return min(at, ROUNDS)


def kernel(
    embed_ref, total_ref, high_ref, table,
    tiles, near, far, row_sums, row_tops, kept_sums, col_sums, col_tops,
    row_lanes, kept_lanes, outbox, inbox,
    own_sem, hop_send, hop_recv, twin_send, twin_recv, post_send, post_recv,
):
    my_row = lax.axis_index("row")
    my_col = lax.axis_index("col")
    z, x_hi = lax.div(my_row, 2), lax.rem(my_row, 2)
    y, x_lo, core = lax.div(my_col, 4), lax.rem(lax.div(my_col, 2), 2), lax.rem(my_col, 2)
    x = x_hi * 2 + x_lo
    other = 1 - core
    chips = {}
    for offset in TILES + DIRECTIONS:
        if offset not in chips:
            px = lax.rem(x + offset[0], 4)
            py = lax.rem(y + offset[1], 4)
            pz = lax.rem(z + offset[2], 4)
            chips[offset] = (pz * 2 + lax.div(px, 2), py * 4 + lax.rem(px, 2) * 2)

    def device(offset, at_core):
        row, col = chips[offset]
        return (row, col + at_core)

    def span(chunk):
        return pl.ds(chunk * PIECE, PIECE)

    def hop(tile, chunk):
        origin = parent(tile, chunk)
        step = DIRECTIONS[ROUTES[tile][chunk]]
        source = embed_ref.at[span(chunk)] if origin == 0 else tiles.at[origin, core, span(chunk)]
        return pltpu.make_async_remote_copy(
            src_ref=source,
            dst_ref=tiles.at[tile, core, span(chunk)],
            send_sem=hop_send,
            recv_sem=hop_recv.at[tile, chunk],
            device_id=device(minus((0, 0, 0), step), core),
            device_id_type=MESH,
        )

    def twin(tile, chunk):
        source = embed_ref.at[span(chunk)] if tile == 0 else tiles.at[tile, core, span(chunk)]
        return pltpu.make_async_remote_copy(
            src_ref=source,
            dst_ref=tiles.at[tile, core, span(chunk)],
            send_sem=twin_send,
            recv_sem=twin_recv.at[tile],
            device_id=device((0, 0, 0), other),
            device_id_type=MESH,
        )

    def twin_whole(tile):
        return pltpu.make_async_remote_copy(
            src_ref=tiles.at[tile, other],
            dst_ref=tiles.at[tile, other],
            send_sem=twin_send,
            recv_sem=twin_recv.at[tile],
            device_id=device((0, 0, 0), other),
            device_id_type=MESH,
        )

    def post(tile, place, at_core):
        return pltpu.make_async_remote_copy(
            src_ref=outbox.at[place],
            dst_ref=inbox.at[place],
            send_sem=post_send,
            recv_sem=post_recv,
            device_id=device(TILES[tile], at_core),
            device_id_type=MESH,
        )

    own = pltpu.make_async_copy(embed_ref, tiles.at[0, core], own_sem)
    own.start()

    barrier = pltpu.get_barrier_semaphore()
    for step in DIRECTIONS:
        pl.semaphore_signal(barrier, inc=1, device_id=device(step, core), device_id_type=MESH)
    pl.semaphore_signal(barrier, inc=1, device_id=device((0, 0, 0), other), device_id_type=MESH)
    pl.semaphore_wait(barrier, 7)

    for tile, chunk in FIRST:
        hop(tile, chunk).start()
    for chunk in range(CHUNKS):
        twin(0, chunk).start()

    row_sums[...] = jnp.zeros_like(row_sums)
    col_sums[...] = jnp.zeros_like(col_sums)
    row_tops[...] = jnp.full_like(row_tops, LOWEST)
    col_tops[...] = jnp.full_like(col_tops, LOWEST)
    far[...] = jnp.zeros_like(far)

    def multiply(target, left, right):
        target[...] = lax.dot_general(
            tiles[left, core], tiles[right].reshape(2 * ROWS, WIDTH), TRANSPOSED,
            preferred_element_type=jnp.float32,
        )

    def halves(op, values):
        return (
            op(values[:, 0:128], values[:, 128:256]),
            op(values[:, 256:384], values[:, 384:512]),
        )

    def reduce(source, row, kept, col, own_pair=False):
        sums = tops = None
        for first in range(0, ROWS, 64):
            part = pl.ds(first, 64)
            scores = source[part, :]
            weights = jnp.exp2(scores * SCALE - SCALE)
            if own_pair:
                place = lax.broadcasted_iota(jnp.int32, (64, 2 * ROWS), 0) + (first + core * ROWS)
                itself = place == lax.broadcasted_iota(jnp.int32, (64, 2 * ROWS), 1)
                weights = jnp.where(itself, 0.0, weights)
                scores = jnp.where(itself, LOWEST, scores)
            left, right = halves(jnp.add, weights)
            row_sums[row, part] += left + right
            kept_sums[kept, part] = jnp.where(core == 0, left, right)
            row_tops[row, part] = jnp.maximum(
                row_tops[row, part], jnp.maximum(*halves(jnp.maximum, scores))
            )
            if own_pair:
                continue
            for at in range(0, 64, 8):
                sums = weights[at:at + 8] if sums is None else sums + weights[at:at + 8]
                high = scores[at:at + 8]
                tops = high if tops is None else jnp.maximum(tops, high)
        if not own_pair:
            col_sums[col] += sums
            col_tops[col] = jnp.maximum(col_tops[col], tops)

    def arrive(tile, chunk):
        hop(tile, chunk).wait_recv()
        for child, piece in CHILDREN.get((tile, chunk), ()):
            hop(child, piece).start()
        if tile in SHARED_TILES:
            twin(tile, chunk).start()

    own.wait()
    twin_whole(0).wait_recv()
    multiply(near, 0, 0)
    reduce(near, 0, SPARE_KEPT + 1, SPARE_COL, own_pair=True)

    def across(values, op):
        return op(values.T, axis=0, keepdims=True)

    def column(values, op, half):
        mine = jnp.where(core == half, values[:, :ROWS], values[:, ROWS:])
        return op(mine, axis=0, keepdims=True)

    def finish(tile):
        places = {0: SAME_CORE[tile]}
        if tile in COL_TILES:
            places[1] = CROSS_CORE[tile]
        for half, place in reversed(places.items()):
            sums = tops = None
            if tile in COL_TILES:
                sums = column(col_sums[tile], jnp.sum, half)
                tops = column(col_tops[tile], jnp.max, half)
            for at, (_, _, right) in enumerate(KEPT):
                if right is not None and right[0] == tile:
                    extra = column(col_sums[KEPT_COL + at], jnp.sum, half)
                    sums = sums + extra
                    tops = jnp.maximum(tops, column(col_tops[KEPT_COL + at], jnp.max, half))
                    if half == 0:
                        outbox[place, pl.ds(right[1], 1), :] = extra
            if half == 0 and (tile in ROW_TILES or tile == 0):
                if LANE_ROWS[tile] < ROUNDS:
                    low, high = row_lanes[tile, 0:1, :], row_lanes[tile, 1:2, :]
                else:
                    low, high = across(row_sums[tile], jnp.sum), across(row_tops[tile], jnp.max)
                sums = low if sums is None else sums + low
                tops = high if tops is None else jnp.maximum(tops, high)
                for at, (_, left, _) in enumerate(KEPT):
                    if left[0] == tile:
                        if LANE_KEPT[at] < ROUNDS:
                            kept = kept_lanes[at, 0:1, :]
                        else:
                            kept = across(kept_sums[at], jnp.sum)
                        outbox[place, pl.ds(left[1], 1), :] = kept
            outbox[place, 0:1, :] = sums
            outbox[place, 1:2, :] = tops
            if place != MESSAGES:
                post(tile, place, other if half else core).start()

    def lanes(row, kept):
        row_lanes[row, 0:1, :] = across(row_sums[row], jnp.sum)
        row_lanes[row, 1:2, :] = across(row_tops[row], jnp.max)
        kept_lanes[kept, 0:1, :] = across(kept_sums[kept], jnp.sum)

    def arrivals(number, second):
        if True:
            step = 2 * number + second
            if step < len(PAIRS):
                for tile, chunk in ARRIVALS[step]:
                    arrive(tile, chunk)
                for tile in SHARED_TILES:
                    if tile != 0 and first_use(tile) == step:
                        twin_whole(tile).wait_recv()
            values = slots(step) if step < len(PAIRS) else NOTHING
            if not second:
                row = [tile for tile, at in LANE_ROWS.items() if at == number] or [SPARE_ROW]
                kept = [place for place, at in LANE_KEPT.items() if at == number] or [SPARE_KEPT]
                values = values + (row[0], kept[0])
                for tile in range(COUNT):
                    if done_round(tile) == number:
                        finish(tile)
            return values

    before = NOTHING[2:5]
    for number in range(ROUNDS):
        one, two = arrivals(number, 0), arrivals(number, 1)
        lanes(*one[5:7])
        multiply(near, one[0], one[1])
        reduce(far, *before)
        multiply(far, two[0], two[1])
        reduce(near, *one[2:5])
        before = two[2:5]
    last = before
    reduce(far, *last)
    for tile in list(range(1, COUNT)) + [0]:
        if done_round(tile) == ROUNDS:
            finish(tile)
    table[0:1, :] = across(kept_sums[SPARE_KEPT + 1], jnp.sum)

    moved = tiles.at[pl.ds(1, COUNT - 1), core]
    pltpu.make_async_copy(moved, moved, hop_send).wait()
    shared = tiles.at[pl.ds(0, len(SHARED_TILES)), core]
    pltpu.make_async_copy(shared, shared, twin_send).wait()
    sent = outbox.at[pl.ds(0, MESSAGES)]
    pltpu.make_async_copy(sent, sent, post_send).wait()
    pltpu.make_async_copy(inbox, inbox, post_recv).wait()

    sums = tops = outbox[MESSAGES]
    for place in range(MESSAGES):
        sums = sums + inbox[place]
        tops = jnp.maximum(tops, inbox[place])
    total_ref[...] = sums
    high_ref[...] = tops
    for _, left, right in KEPT:
        for side in (left, right):
            if side is not None:
                where = outbox if side[0] == 0 else inbox
                table[pl.ds(side[2], 1), :] = where[SAME_CORE[side[0]], pl.ds(side[1], 1), :]

def finisher(cand_ref, total_ref, high_ref, table_ref, counts_ref, tops_ref, recount_ref):
    my_row = lax.axis_index("row")
    z, x_hi = my_row // 2, my_row % 2
    counts_ref[...] = total_ref[0, :]
    tops_ref[...] = high_ref[1, :]
    for number in range(2):
        chosen = cand_ref[number]
        apart = ((chosen // 2 - z + 4) % 4) * 2 + (chosen % 2 - x_hi + 2) % 2
        recount_ref[pl.ds(number, 1), :] = table_ref[pl.ds(apart, 1), :]


def per_device(embed, cand_tiles):
    vector = pltpu.VMEM
    semaphores = pltpu.SemaphoreType.DMA
    in_vector = pl.BlockSpec(memory_space=pltpu.VMEM)
    parts = pl.pallas_call(
        kernel,
        out_shape=(jax.ShapeDtypeStruct((8, ROWS), jnp.float32),) * 3,
        in_specs=[pl.BlockSpec(memory_space=pl.ANY)],
        out_specs=[in_vector] * 3,
        scratch_shapes=[
            vector((COUNT, 2, ROWS, WIDTH), jnp.bfloat16),
            vector((ROWS, 2 * ROWS), jnp.float32),
            vector((ROWS, 2 * ROWS), jnp.float32),
            vector((COUNT + 1, ROWS, 128), jnp.float32),
            vector((COUNT + 1, ROWS, 128), jnp.float32),
            vector((SPARE_KEPT + 2, ROWS, 128), jnp.float32),
            vector((KEPT_COL + len(KEPT), 8, 2 * ROWS), jnp.float32),
            vector((KEPT_COL + len(KEPT), 8, 2 * ROWS), jnp.float32),
            vector((COUNT + 1, 8, ROWS), jnp.float32),
            vector((SPARE_KEPT + 1, 8, ROWS), jnp.float32),
            vector((MESSAGES + 1, 8, ROWS), jnp.float32),
            vector((MESSAGES, 8, ROWS), jnp.float32),
            semaphores,
            semaphores,
            semaphores((COUNT, CHUNKS)),
            semaphores,
            semaphores((COUNT,)),
            semaphores,
            semaphores,
        ],
        compiler_params=pltpu.CompilerParams(
            collective_id=0, has_side_effects=True, vmem_limit_bytes=56 * 1024 * 1024
        ),
        cost_estimate=pl.CostEstimate(
            flops=37 * 2 * ROWS * 2 * ROWS * WIDTH,
            bytes_accessed=COUNT * 2 * ROWS * WIDTH * 2,
            transcendentals=37 * ROWS * 2 * ROWS,
        ),
    )(embed)
    return pl.pallas_call(
        finisher,
        out_shape=(
            jax.ShapeDtypeStruct((ROWS,), jnp.float32),
            jax.ShapeDtypeStruct((ROWS,), jnp.float32),
            jax.ShapeDtypeStruct((2, ROWS), jnp.float32),
        ),
        in_specs=[pl.BlockSpec(memory_space=pltpu.SMEM)] + [in_vector] * 3,
        out_specs=[in_vector] * 3,
    )(cand_tiles, *parts)


def solution(mesh):
    in_specs = (P(("row", "col"), None), P(("row", "col")))
    out_specs = (P(("row", "col")), P(("row", "col")), P(("row", "col"), None))
    return jax.shard_map(
        per_device, mesh=mesh, in_specs=in_specs, out_specs=out_specs, check_vma=False
    )
```

```python
import jax
import jax.numpy as jnp
from jax import lax
from jax.experimental import pallas as pl
from jax.experimental.pallas import tpu as pltpu
from jax.sharding import PartitionSpec as P

MESH = pl.DeviceIdType.MESH
ROWS = 256
WIDTH = 768
SCALE = 20.0 * 1.4426950408889634
LOWEST = -3.0
TRANSPOSED = (((1,), (1,)), ((), ()))
DIRECTIONS = ((1, 0, 0), (3, 0, 0), (0, 1, 0), (0, 3, 0), (0, 0, 1), (0, 0, 3))
CHUNKS = 4
TILES = (
   (0, 0, 0),
   (0, 0, 1),
   (0, 0, 2),
   (0, 1, 0),
   (0, 1, 2),
   (0, 1, 3),
   (0, 3, 0),
   (1, 0, 0),
   (2, 0, 0),
   (2, 3, 0),
   (3, 0, 0),
   (3, 2, 0),
   (3, 3, 0),
)
ROUTES = (
    (),
   (4, 4, 4, 4),
   (4, 4, 4, 4),
   (2, 2, 2, 2),
   (5, 2, 2, 5),
   (5, 5, 5, 5),
   (3, 3, 0, 3),
   (0, 0, 0, 0),
   (0, 0, 1, 1),
   (1, 1, 1, 1),
   (2, 2, 1, 1),
   (3, 3, 3, 3),
   (1, 1, 3, 3),
)
FIRST = ((1, 0), (3, 2), (6, 0), (7, 2), (10, 2), (1, 1), (3, 3), (6, 1), (7, 3), (10, 3), (1, 2), (3, 0), (6, 3), (7, 0), (1, 3), (3, 1), (7, 1),)
PAIRS = (
   (1, 0, 0),
   (3, 0, 0),
   (7, 0, 0),
   (3, 7, 0),
   (1, 3, 0),
   (1, 7, 0),
   (12, 7, 0),
   (12, 3, 0),
   (12, 1, 0),
   (12, 0, 0),
   (5, 1, 0),
   (8, 1, 0),
   (8, 0, 1),
   (5, 12, 0),
   (5, 7, 0),
   (5, 8, 0),
   (6, 5, 0),
   (6, 3, 1),
   (6, 1, 0),
   (10, 1, 0),
   (10, 5, 0),
   (2, 0, 1),
   (2, 8, 1),
   (2, 12, 0),
   (2, 7, 0),
   (11, 5, 0),
   (11, 2, 0),
   (11, 1, 0),
   (11, 7, 1),
   (4, 7, 0),
   (4, 8, 0),
   (4, 6, 1),
   (9, 1, 0),
   (9, 5, 0),
   (9, 4, 1),
)
ARRIVALS = (
    ((1, 0), (3, 2), (6, 0), (7, 2), (10, 2), (1, 1), (3, 3), (6, 1), (7, 3), (10, 3), (1, 2), (3, 0), (6, 3), (7, 0), (5, 2), (12, 0), (1, 3), (3, 1), (7, 1), (12, 2),),
    ((5, 3), (8, 2),),
    (),
    (),
    (),
    ((2, 0), (12, 3),),
    ((5, 0), (8, 0), (12, 1),),
    ((10, 0),),
    (),
    (),
    ((2, 1), (11, 0), (5, 1), (8, 1), (8, 3),),
    (),
    (),
    (),
    ((2, 2), (11, 2),),
    ((4, 3), (6, 2), (9, 0),),
    ((10, 1),),
    (),
    (),
    ((2, 3), (11, 3),),
    ((4, 0), (9, 2),),
    ((4, 1),),
    (),
    (),
    ((11, 1),),
    ((9, 3),),
    ((4, 2),),
    (),
    (),
    (),
    (),
    ((9, 1),),
    (),
    (),
    (),
)
COUNT = len(TILES)
PIECE = ROWS // CHUNKS


def minus(a, b):
    return tuple((p - q) % 4 for p, q in zip(a, b))


def parent(tile, chunk):
    return TILES.index(minus(TILES[tile], DIRECTIONS[ROUTES[tile][chunk]]))


def children():
    table = {}
    for tile in range(1, COUNT):
        for chunk in range(CHUNKS):
            table.setdefault((parent(tile, chunk), chunk), []).append((tile, chunk))
    return table


CHILDREN = children()
ROW_TILES = sorted({x for x, _, _ in PAIRS})
SHARED_TILES = sorted({y for _, y, _ in PAIRS} | {0})
COL_TILES = sorted({y for _, y, one in PAIRS if not one})


def kept_rows():
    kept = []
    fill = [2] * COUNT
    for number, (x, y, one) in enumerate(PAIRS):
        apart = minus(TILES[y], TILES[x])
        if apart[1] == 0 and apart[0] % 2 == 0:
            back = minus(TILES[x], TILES[y])
            left = (x, fill[x], apart[2] * 2 + apart[0] // 2)
            fill[x] += 1
            right = None
            if not one:
                right = (y, fill[y], back[2] * 2 + back[0] // 2)
                fill[y] += 1
            kept.append((number, left, right))
    return kept


KEPT = kept_rows()
KEPT_OF = {number: place for place, (number, _, _) in enumerate(KEPT)}
SPARE_ROW = COUNT
SPARE_KEPT = len(KEPT)
SPARE_COL = COUNT
KEPT_COL = COUNT + 1


def slots(number):
    x, y, one = PAIRS[number]
    kept = KEPT_OF.get(number, SPARE_KEPT)
    if one:
        col = SPARE_COL
    elif kept != SPARE_KEPT:
        col = KEPT_COL + kept
    else:
        col = y
    return (x, y, x, kept, col)


NOTHING = (0, 0, SPARE_ROW, SPARE_KEPT, SPARE_COL)
ROUNDS = (len(PAIRS) + 1) // 2


def first_use(tile):
    for number, (_, y, _) in enumerate(PAIRS):
        if y == tile:
            return number
    return None


SAME_CORE = {tile: place for place, tile in enumerate(range(1, COUNT))}
CROSS_CORE = {tile: len(SAME_CORE) + place for place, tile in enumerate(COL_TILES)}
MESSAGES = len(SAME_CORE) + len(CROSS_CORE)
SAME_CORE[0] = MESSAGES


def last_round(tile, cols):
    steps = [n for n, (x, y, one) in enumerate(PAIRS) if x == tile or (cols and y == tile and not one)]
    last = max(steps, default=-1)
    return 0 if last < 0 else last // 2 + last % 2


def lane_rounds():
    rows, kept, free = {}, {}, {}
    for tile in sorted(ROW_TILES + ([] if 0 in ROW_TILES else [0]), key=lambda t: last_round(t, False)):
        at = last_round(tile, False) + 1
        while at in free:
            at += 1
        free[at] = tile
        rows[tile] = at
    used = set()
    for place, (number, _, _) in enumerate(KEPT):
        at = number // 2 + number % 2 + 1
        while at in used:
            at += 1
        used.add(at)
        kept[place] = at
    return rows, kept


LANE_ROWS, LANE_KEPT = lane_rounds()


def done_round(tile):
    at = last_round(tile, True) + 1
    if LANE_ROWS.get(tile, -1) < ROUNDS:
        at = max(at, LANE_ROWS.get(tile, -1) + 1)
    for place, (_, left, _) in enumerate(KEPT):
        if left[0] == tile and LANE_KEPT[place] < ROUNDS:
            at = max(at, LANE_KEPT[place] + 1)
    if LANE_ROWS.get(tile, -1) >= ROUNDS:
        at = ROUNDS
    for place, (_, left, _) in enumerate(KEPT):
        if left[0] == tile and LANE_KEPT[place] >= ROUNDS:
            at = ROUNDS
    return min(at, ROUNDS)


def kernel(
    embed_ref, total_ref, high_ref, table,
    tiles, near, far, row_sums, row_tops, kept_sums, col_sums, col_tops,
    row_lanes, kept_lanes, outbox, inbox,
    own_sem, hop_send, hop_recv, twin_send, twin_recv, post_send, post_recv,
):
    my_row = lax.axis_index("row")
    my_col = lax.axis_index("col")
    z, x_hi = lax.div(my_row, 2), lax.rem(my_row, 2)
    y, x_lo, core = lax.div(my_col, 4), lax.rem(lax.div(my_col, 2), 2), lax.rem(my_col, 2)
    x = x_hi * 2 + x_lo
    other = 1 - core
    chips = {}
    for offset in TILES + DIRECTIONS:
        if offset not in chips:
            px = lax.rem(x + offset[0], 4)
            py = lax.rem(y + offset[1], 4)
            pz = lax.rem(z + offset[2], 4)
            chips[offset] = (pz * 2 + lax.div(px, 2), py * 4 + lax.rem(px, 2) * 2)

    def device(offset, at_core):
        row, col = chips[offset]
        return (row, col + at_core)

    def span(chunk):
        return pl.ds(chunk * PIECE, PIECE)

    def hop(tile, chunk):
        origin = parent(tile, chunk)
        step = DIRECTIONS[ROUTES[tile][chunk]]
        source = embed_ref.at[span(chunk)] if origin == 0 else tiles.at[origin, core, span(chunk)]
        return pltpu.make_async_remote_copy(
            src_ref=source,
            dst_ref=tiles.at[tile, core, span(chunk)],
            send_sem=hop_send,
            recv_sem=hop_recv.at[tile, chunk],
            device_id=device(minus((0, 0, 0), step), core),
            device_id_type=MESH,
        )

    def twin(tile, chunk):
        source = embed_ref.at[span(chunk)] if tile == 0 else tiles.at[tile, core, span(chunk)]
        return pltpu.make_async_remote_copy(
            src_ref=source,
            dst_ref=tiles.at[tile, core, span(chunk)],
            send_sem=twin_send,
            recv_sem=twin_recv.at[tile],
            device_id=device((0, 0, 0), other),
            device_id_type=MESH,
        )

    def twin_whole(tile):
        return pltpu.make_async_remote_copy(
            src_ref=tiles.at[tile, other],
            dst_ref=tiles.at[tile, other],
            send_sem=twin_send,
            recv_sem=twin_recv.at[tile],
            device_id=device((0, 0, 0), other),
            device_id_type=MESH,
        )

    def post(tile, place, at_core):
        return pltpu.make_async_remote_copy(
            src_ref=outbox.at[place],
            dst_ref=inbox.at[place],
            send_sem=post_send,
            recv_sem=post_recv,
            device_id=device(TILES[tile], at_core),
            device_id_type=MESH,
        )

    own = pltpu.make_async_copy(embed_ref, tiles.at[0, core], own_sem)
    own.start()

    barrier = pltpu.get_barrier_semaphore()
    for step in DIRECTIONS:
        pl.semaphore_signal(barrier, inc=1, device_id=device(step, core), device_id_type=MESH)
    pl.semaphore_signal(barrier, inc=1, device_id=device((0, 0, 0), other), device_id_type=MESH)
    pl.semaphore_wait(barrier, 7)

    for tile, chunk in FIRST:
        hop(tile, chunk).start()
    for chunk in range(CHUNKS):
        twin(0, chunk).start()

    row_sums[...] = jnp.zeros_like(row_sums)
    col_sums[...] = jnp.zeros_like(col_sums)
    row_tops[...] = jnp.full_like(row_tops, LOWEST)
    col_tops[...] = jnp.full_like(col_tops, LOWEST)
    far[...] = jnp.zeros_like(far)

    def multiply(target, left, right):
        target[...] = lax.dot_general(
            tiles[left, core], tiles[right].reshape(2 * ROWS, WIDTH), TRANSPOSED,
            preferred_element_type=jnp.float32,
        )

    def halves(op, values):
        return (
            op(values[:, 0:128], values[:, 128:256]),
            op(values[:, 256:384], values[:, 384:512]),
        )

    def reduce(source, row, kept, col, own_pair=False):
        sums = tops = None
        for first in range(0, ROWS, 64):
            part = pl.ds(first, 64)
            scores = source[part, :]
            weights = jnp.exp2(scores * SCALE - SCALE)
            if own_pair:
                place = lax.broadcasted_iota(jnp.int32, (64, 2 * ROWS), 0) + (first + core * ROWS)
                itself = place == lax.broadcasted_iota(jnp.int32, (64, 2 * ROWS), 1)
                weights = jnp.where(itself, 0.0, weights)
                scores = jnp.where(itself, LOWEST, scores)
            left, right = halves(jnp.add, weights)
            row_sums[row, part] += left + right
            kept_sums[kept, part] = jnp.where(core == 0, left, right)
            row_tops[row, part] = jnp.maximum(
                row_tops[row, part], jnp.maximum(*halves(jnp.maximum, scores))
            )
            if own_pair:
                continue
            for at in range(0, 64, 8):
                sums = weights[at:at + 8] if sums is None else sums + weights[at:at + 8]
                high = scores[at:at + 8]
                tops = high if tops is None else jnp.maximum(tops, high)
        if not own_pair:
            col_sums[col] += sums
            col_tops[col] = jnp.maximum(col_tops[col], tops)

    def arrive(tile, chunk):
        hop(tile, chunk).wait_recv()
        for child, piece in CHILDREN.get((tile, chunk), ()):
            hop(child, piece).start()
        if tile in SHARED_TILES:
            twin(tile, chunk).start()

    own.wait()
    twin_whole(0).wait_recv()
    multiply(near, 0, 0)
    reduce(near, 0, SPARE_KEPT + 1, SPARE_COL, own_pair=True)

    def across(values, op):
        return op(values.T, axis=0, keepdims=True)

    def column(values, op, half):
        mine = jnp.where(core == half, values[:, :ROWS], values[:, ROWS:])
        return op(mine, axis=0, keepdims=True)

    def finish(tile):
        places = {0: SAME_CORE[tile]}
        if tile in COL_TILES:
            places[1] = CROSS_CORE[tile]
        for half, place in reversed(places.items()):
            sums = tops = None
            if tile in COL_TILES:
                sums = column(col_sums[tile], jnp.sum, half)
                tops = column(col_tops[tile], jnp.max, half)
            for at, (_, _, right) in enumerate(KEPT):
                if right is not None and right[0] == tile:
                    extra = column(col_sums[KEPT_COL + at], jnp.sum, half)
                    sums = sums + extra
                    tops = jnp.maximum(tops, column(col_tops[KEPT_COL + at], jnp.max, half))
                    if half == 0:
                        outbox[place, pl.ds(right[1], 1), :] = extra
            if half == 0 and (tile in ROW_TILES or tile == 0):
                if LANE_ROWS[tile] < ROUNDS:
                    low, high = row_lanes[tile, 0:1, :], row_lanes[tile, 1:2, :]
                else:
                    low, high = across(row_sums[tile], jnp.sum), across(row_tops[tile], jnp.max)
                sums = low if sums is None else sums + low
                tops = high if tops is None else jnp.maximum(tops, high)
                for at, (_, left, _) in enumerate(KEPT):
                    if left[0] == tile:
                        if LANE_KEPT[at] < ROUNDS:
                            kept = kept_lanes[at, 0:1, :]
                        else:
                            kept = across(kept_sums[at], jnp.sum)
                        outbox[place, pl.ds(left[1], 1), :] = kept
            outbox[place, 0:1, :] = sums
            outbox[place, 1:2, :] = tops
            if place != MESSAGES:
                post(tile, place, other if half else core).start()

    def lanes(row, kept):
        row_lanes[row, 0:1, :] = across(row_sums[row], jnp.sum)
        row_lanes[row, 1:2, :] = across(row_tops[row], jnp.max)
        kept_lanes[kept, 0:1, :] = across(kept_sums[kept], jnp.sum)

    def arrivals(number, second):
        if True:
            step = 2 * number + second
            if step < len(PAIRS):
                for tile, chunk in ARRIVALS[step]:
                    arrive(tile, chunk)
                for tile in SHARED_TILES:
                    if tile != 0 and first_use(tile) == step:
                        twin_whole(tile).wait_recv()
            values = slots(step) if step < len(PAIRS) else NOTHING
            if not second:
                row = [tile for tile, at in LANE_ROWS.items() if at == number] or [SPARE_ROW]
                kept = [place for place, at in LANE_KEPT.items() if at == number] or [SPARE_KEPT]
                values = values + (row[0], kept[0])
                for tile in range(COUNT):
                    if done_round(tile) == number:
                        finish(tile)
            return values

    before = NOTHING[2:5]
    for number in range(ROUNDS):
        one, two = arrivals(number, 0), arrivals(number, 1)
        lanes(*one[5:7])
        multiply(near, one[0], one[1])
        reduce(far, *before)
        multiply(far, two[0], two[1])
        reduce(near, *one[2:5])
        before = two[2:5]
    last = before
    reduce(far, *last)
    for tile in list(range(1, COUNT)) + [0]:
        if done_round(tile) == ROUNDS:
            finish(tile)
    table[0:1, :] = across(kept_sums[SPARE_KEPT + 1], jnp.sum)

    moved = tiles.at[pl.ds(1, COUNT - 1), core]
    pltpu.make_async_copy(moved, moved, hop_send).wait()
    shared = tiles.at[pl.ds(0, len(SHARED_TILES)), core]
    pltpu.make_async_copy(shared, shared, twin_send).wait()
    sent = outbox.at[pl.ds(0, MESSAGES)]
    pltpu.make_async_copy(sent, sent, post_send).wait()
    pltpu.make_async_copy(inbox, inbox, post_recv).wait()

    sums = tops = outbox[MESSAGES]
    for place in range(MESSAGES):
        sums = sums + inbox[place]
        tops = jnp.maximum(tops, inbox[place])
    total_ref[...] = sums
    high_ref[...] = tops
    for _, left, right in KEPT:
        for side in (left, right):
            if side is not None:
                where = outbox if side[0] == 0 else inbox
                table[pl.ds(side[2], 1), :] = where[SAME_CORE[side[0]], pl.ds(side[1], 1), :]

def finisher(cand_ref, total_ref, high_ref, table_ref, counts_ref, tops_ref, recount_ref):
    my_row = lax.axis_index("row")
    z, x_hi = my_row // 2, my_row % 2
    counts_ref[...] = total_ref[0, :]
    tops_ref[...] = high_ref[1, :]
    for number in range(2):
        chosen = cand_ref[number]
        apart = ((chosen // 2 - z + 4) % 4) * 2 + (chosen % 2 - x_hi + 2) % 2
        recount_ref[pl.ds(number, 1), :] = table_ref[pl.ds(apart, 1), :]


def per_device(embed, cand_tiles):
    vector = pltpu.VMEM
    semaphores = pltpu.SemaphoreType.DMA
    in_vector = pl.BlockSpec(memory_space=pltpu.VMEM)
    parts = pl.pallas_call(
        kernel,
        out_shape=(jax.ShapeDtypeStruct((8, ROWS), jnp.float32),) * 3,
        in_specs=[pl.BlockSpec(memory_space=pl.ANY)],
        out_specs=[in_vector] * 3,
        scratch_shapes=[
            vector((COUNT, 2, ROWS, WIDTH), jnp.bfloat16),
            vector((ROWS, 2 * ROWS), jnp.float32),
            vector((ROWS, 2 * ROWS), jnp.float32),
            vector((COUNT + 1, ROWS, 128), jnp.float32),
            vector((COUNT + 1, ROWS, 128), jnp.float32),
            vector((SPARE_KEPT + 2, ROWS, 128), jnp.float32),
            vector((KEPT_COL + len(KEPT), 8, 2 * ROWS), jnp.float32),
            vector((KEPT_COL + len(KEPT), 8, 2 * ROWS), jnp.float32),
            vector((COUNT + 1, 8, ROWS), jnp.float32),
            vector((SPARE_KEPT + 1, 8, ROWS), jnp.float32),
            vector((MESSAGES + 1, 8, ROWS), jnp.float32),
            vector((MESSAGES, 8, ROWS), jnp.float32),
            semaphores,
            semaphores,
            semaphores((COUNT, CHUNKS)),
            semaphores,
            semaphores((COUNT,)),
            semaphores,
            semaphores,
        ],
        compiler_params=pltpu.CompilerParams(
            collective_id=0, has_side_effects=True, vmem_limit_bytes=56 * 1024 * 1024
        ),
        cost_estimate=pl.CostEstimate(
            flops=37 * 2 * ROWS * 2 * ROWS * WIDTH,
            bytes_accessed=COUNT * 2 * ROWS * WIDTH * 2,
            transcendentals=37 * ROWS * 2 * ROWS,
        ),
    )(embed)
    return pl.pallas_call(
        finisher,
        out_shape=(
            jax.ShapeDtypeStruct((ROWS,), jnp.float32),
            jax.ShapeDtypeStruct((ROWS,), jnp.float32),
            jax.ShapeDtypeStruct((2, ROWS), jnp.float32),
        ),
        in_specs=[pl.BlockSpec(memory_space=pltpu.SMEM)] + [in_vector] * 3,
        out_specs=[in_vector] * 3,
    )(cand_tiles, *parts)


def solution(mesh):
    in_specs = (P(("row", "col"), None), P(("row", "col")))
    out_specs = (P(("row", "col")), P(("row", "col")), P(("row", "col"), None))
    return jax.shard_map(
        per_device, mesh=mesh, in_specs=in_specs, out_specs=out_specs, check_vma=False
    )
```

```python
import jax
import jax.numpy as jnp
from jax import lax
from jax.experimental import pallas as pl
from jax.experimental.pallas import tpu as pltpu
from jax.sharding import PartitionSpec as P

MESH = pl.DeviceIdType.MESH
ROWS = 256
WIDTH = 768
SCALE = 20.0 * 1.4426950408889634
LOWEST = -3.0
TRANSPOSED = (((1,), (1,)), ((), ()))
DIRECTIONS = ((1, 0, 0), (3, 0, 0), (0, 1, 0), (0, 3, 0), (0, 0, 1), (0, 0, 3))
CHUNKS = 4
TILES = (
   (0, 0, 0),
   (0, 0, 1),
   (0, 0, 2),
   (0, 1, 0),
   (0, 1, 2),
   (0, 1, 3),
   (0, 3, 0),
   (1, 0, 0),
   (2, 0, 0),
   (2, 3, 0),
   (3, 0, 0),
   (3, 2, 0),
   (3, 3, 0),
)
ROUTES = (
    (),
   (4, 4, 4, 4),
   (4, 4, 4, 4),
   (2, 2, 2, 2),
   (5, 5, 2, 2),
   (5, 5, 5, 5),
   (3, 3, 3, 3),
   (0, 0, 0, 0),
   (0, 0, 0, 0),
   (1, 1, 1, 1),
   (2, 2, 1, 1),
   (3, 3, 3, 3),
   (1, 1, 1, 3),
)
FIRST = ((1, 2), (3, 2), (6, 0), (7, 0), (10, 2), (1, 3), (3, 3), (6, 1), (7, 1), (10, 3), (1, 0), (3, 0), (6, 2), (7, 2), (1, 1), (3, 1), (6, 3), (7, 3),)
PAIRS = (
   (1, 0, 0),
   (3, 0, 0),
   (7, 0, 0),
   (3, 7, 0),
   (6, 7, 0),
   (1, 7, 0),
   (3, 6, 1),
   (1, 3, 0),
   (1, 6, 0),
   (12, 7, 0),
   (12, 1, 0),
   (12, 3, 0),
   (5, 6, 0),
   (5, 1, 0),
   (5, 7, 0),
   (5, 12, 0),
   (10, 1, 0),
   (10, 7, 1),
   (10, 5, 0),
   (8, 5, 0),
   (8, 1, 0),
   (2, 0, 1),
   (2, 12, 0),
   (2, 7, 0),
   (4, 12, 0),
   (4, 7, 0),
   (4, 6, 1),
   (2, 8, 1),
   (4, 8, 0),
   (11, 5, 0),
   (11, 1, 0),
   (11, 7, 1),
   (9, 1, 0),
   (9, 5, 0),
   (9, 4, 1),
)
ARRIVALS = (
    ((1, 2), (3, 2), (6, 0), (7, 0), (10, 2), (1, 3), (3, 3), (6, 1), (7, 1), (10, 3), (1, 0), (3, 0), (6, 2), (7, 2), (5, 2), (12, 0), (1, 1), (3, 1), (6, 3), (7, 3),),
    ((5, 3), (12, 1),),
    (),
    (),
    ((2, 2), (8, 0), (12, 3),),
    ((5, 0), (12, 2),),
    ((10, 0),),
    (),
    (),
    ((2, 3), (8, 1), (11, 0),),
    ((5, 1), (9, 0),),
    ((10, 1),),
    (),
    (),
    ((2, 0), (8, 2), (11, 1),),
    ((9, 1),),
    ((4, 0), (4, 2),),
    (),
    ((2, 1), (8, 3), (11, 3),),
    ((9, 3),),
    ((4, 1), (4, 3),),
    (),
    (),
    ((11, 2),),
    ((9, 2),),
    (),
    (),
    (),
    (),
    (),
    (),
    (),
    (),
    (),
    (),
)
COUNT = len(TILES)
PIECE = ROWS // CHUNKS


def minus(a, b):
    return tuple((p - q) % 4 for p, q in zip(a, b))


def parent(tile, chunk):
    return TILES.index(minus(TILES[tile], DIRECTIONS[ROUTES[tile][chunk]]))


def children():
    table = {}
    for tile in range(1, COUNT):
        for chunk in range(CHUNKS):
            table.setdefault((parent(tile, chunk), chunk), []).append((tile, chunk))
    return table


CHILDREN = children()
ROW_TILES = sorted({x for x, _, _ in PAIRS})
SHARED_TILES = sorted({y for _, y, _ in PAIRS} | {0})
COL_TILES = sorted({y for _, y, one in PAIRS if not one})


def kept_rows():
    kept = []
    fill = [2] * COUNT
    for number, (x, y, one) in enumerate(PAIRS):
        apart = minus(TILES[y], TILES[x])
        if apart[1] == 0 and apart[0] % 2 == 0:
            back = minus(TILES[x], TILES[y])
            left = (x, fill[x], apart[2] * 2 + apart[0] // 2)
            fill[x] += 1
            right = None
            if not one:
                right = (y, fill[y], back[2] * 2 + back[0] // 2)
                fill[y] += 1
            kept.append((number, left, right))
    return kept


KEPT = kept_rows()
KEPT_OF = {number: place for place, (number, _, _) in enumerate(KEPT)}
SPARE_ROW = COUNT
SPARE_KEPT = len(KEPT)
SPARE_COL = COUNT
KEPT_COL = COUNT + 1


def slots(number):
    x, y, one = PAIRS[number]
    kept = KEPT_OF.get(number, SPARE_KEPT)
    if one:
        col = SPARE_COL
    elif kept != SPARE_KEPT:
        col = KEPT_COL + kept
    else:
        col = y
    return (x, y, x, kept, col)


NOTHING = (0, 0, SPARE_ROW, SPARE_KEPT, SPARE_COL)
ROUNDS = (len(PAIRS) + 1) // 2


def first_use(tile):
    for number, (_, y, _) in enumerate(PAIRS):
        if y == tile:
            return number
    return None


SAME_CORE = {tile: place for place, tile in enumerate(range(1, COUNT))}
CROSS_CORE = {tile: len(SAME_CORE) + place for place, tile in enumerate(COL_TILES)}
MESSAGES = len(SAME_CORE) + len(CROSS_CORE)
SAME_CORE[0] = MESSAGES


def last_round(tile, cols):
    steps = [n for n, (x, y, one) in enumerate(PAIRS) if x == tile or (cols and y == tile and not one)]
    last = max(steps, default=-1)
    return 0 if last < 0 else last // 2 + last % 2


def lane_rounds():
    rows, kept, free = {}, {}, {}
    for tile in sorted(ROW_TILES + ([] if 0 in ROW_TILES else [0]), key=lambda t: last_round(t, False)):
        at = last_round(tile, False) + 1
        while at in free:
            at += 1
        free[at] = tile
        rows[tile] = at
    used = set()
    for place, (number, _, _) in enumerate(KEPT):
        at = number // 2 + number % 2 + 1
        while at in used:
            at += 1
        used.add(at)
        kept[place] = at
    return rows, kept


LANE_ROWS, LANE_KEPT = lane_rounds()


def done_round(tile):
    at = last_round(tile, True) + 1
    if LANE_ROWS.get(tile, -1) < ROUNDS:
        at = max(at, LANE_ROWS.get(tile, -1) + 1)
    for place, (_, left, _) in enumerate(KEPT):
        if left[0] == tile and LANE_KEPT[place] < ROUNDS:
            at = max(at, LANE_KEPT[place] + 1)
    if LANE_ROWS.get(tile, -1) >= ROUNDS:
        at = ROUNDS
    for place, (_, left, _) in enumerate(KEPT):
        if left[0] == tile and LANE_KEPT[place] >= ROUNDS:
            at = ROUNDS
    return min(at, ROUNDS)


def kernel(
    embed_ref, total_ref, high_ref, table,
    tiles, near, far, row_sums, row_tops, kept_sums, col_sums, col_tops,
    row_lanes, kept_lanes, outbox, inbox,
    own_sem, hop_send, hop_recv, twin_send, twin_recv, post_send, post_recv,
):
    my_row = lax.axis_index("row")
    my_col = lax.axis_index("col")
    z, x_hi = lax.div(my_row, 2), lax.rem(my_row, 2)
    y, x_lo, core = lax.div(my_col, 4), lax.rem(lax.div(my_col, 2), 2), lax.rem(my_col, 2)
    x = x_hi * 2 + x_lo
    other = 1 - core
    chips = {}
    for offset in TILES + DIRECTIONS:
        if offset not in chips:
            px = lax.rem(x + offset[0], 4)
            py = lax.rem(y + offset[1], 4)
            pz = lax.rem(z + offset[2], 4)
            chips[offset] = (pz * 2 + lax.div(px, 2), py * 4 + lax.rem(px, 2) * 2)

    def device(offset, at_core):
        row, col = chips[offset]
        return (row, col + at_core)

    def span(chunk):
        return pl.ds(chunk * PIECE, PIECE)

    def hop(tile, chunk):
        origin = parent(tile, chunk)
        step = DIRECTIONS[ROUTES[tile][chunk]]
        source = embed_ref.at[span(chunk)] if origin == 0 else tiles.at[origin, core, span(chunk)]
        return pltpu.make_async_remote_copy(
            src_ref=source,
            dst_ref=tiles.at[tile, core, span(chunk)],
            send_sem=hop_send,
            recv_sem=hop_recv.at[tile, chunk],
            device_id=device(minus((0, 0, 0), step), core),
            device_id_type=MESH,
        )

    def twin(tile, chunk):
        source = embed_ref.at[span(chunk)] if tile == 0 else tiles.at[tile, core, span(chunk)]
        return pltpu.make_async_remote_copy(
            src_ref=source,
            dst_ref=tiles.at[tile, core, span(chunk)],
            send_sem=twin_send,
            recv_sem=twin_recv.at[tile],
            device_id=device((0, 0, 0), other),
            device_id_type=MESH,
        )

    def twin_whole(tile):
        return pltpu.make_async_remote_copy(
            src_ref=tiles.at[tile, other],
            dst_ref=tiles.at[tile, other],
            send_sem=twin_send,
            recv_sem=twin_recv.at[tile],
            device_id=device((0, 0, 0), other),
            device_id_type=MESH,
        )

    def post(tile, place, at_core):
        return pltpu.make_async_remote_copy(
            src_ref=outbox.at[place],
            dst_ref=inbox.at[place],
            send_sem=post_send,
            recv_sem=post_recv,
            device_id=device(TILES[tile], at_core),
            device_id_type=MESH,
        )

    own = pltpu.make_async_copy(embed_ref, tiles.at[0, core], own_sem)
    own.start()

    barrier = pltpu.get_barrier_semaphore()
    for step in DIRECTIONS:
        pl.semaphore_signal(barrier, inc=1, device_id=device(step, core), device_id_type=MESH)
    pl.semaphore_signal(barrier, inc=1, device_id=device((0, 0, 0), other), device_id_type=MESH)
    pl.semaphore_wait(barrier, 7)

    for tile, chunk in FIRST:
        hop(tile, chunk).start()
    for chunk in range(CHUNKS):
        twin(0, chunk).start()

    row_sums[...] = jnp.zeros_like(row_sums)
    col_sums[...] = jnp.zeros_like(col_sums)
    row_tops[...] = jnp.full_like(row_tops, LOWEST)
    col_tops[...] = jnp.full_like(col_tops, LOWEST)
    far[...] = jnp.zeros_like(far)

    def multiply(target, left, right):
        target[...] = lax.dot_general(
            tiles[left, core], tiles[right].reshape(2 * ROWS, WIDTH), TRANSPOSED,
            preferred_element_type=jnp.float32,
        )

    def halves(op, values):
        return (
            op(values[:, 0:128], values[:, 128:256]),
            op(values[:, 256:384], values[:, 384:512]),
        )

    def reduce(source, row, kept, col, own_pair=False):
        sums = tops = None
        for first in range(0, ROWS, 64):
            part = pl.ds(first, 64)
            scores = source[part, :]
            weights = jnp.exp2(scores * SCALE - SCALE)
            if own_pair:
                place = lax.broadcasted_iota(jnp.int32, (64, 2 * ROWS), 0) + (first + core * ROWS)
                itself = place == lax.broadcasted_iota(jnp.int32, (64, 2 * ROWS), 1)
                weights = jnp.where(itself, 0.0, weights)
                scores = jnp.where(itself, LOWEST, scores)
            left, right = halves(jnp.add, weights)
            row_sums[row, part] += left + right
            kept_sums[kept, part] = jnp.where(core == 0, left, right)
            row_tops[row, part] = jnp.maximum(
                row_tops[row, part], jnp.maximum(*halves(jnp.maximum, scores))
            )
            if own_pair:
                continue
            for at in range(0, 64, 8):
                sums = weights[at:at + 8] if sums is None else sums + weights[at:at + 8]
                high = scores[at:at + 8]
                tops = high if tops is None else jnp.maximum(tops, high)
        if not own_pair:
            col_sums[col] += sums
            col_tops[col] = jnp.maximum(col_tops[col], tops)

    def arrive(tile, chunk):
        hop(tile, chunk).wait_recv()
        for child, piece in CHILDREN.get((tile, chunk), ()):
            hop(child, piece).start()
        if tile in SHARED_TILES:
            twin(tile, chunk).start()

    own.wait()
    twin_whole(0).wait_recv()
    multiply(near, 0, 0)
    reduce(near, 0, SPARE_KEPT + 1, SPARE_COL, own_pair=True)

    def across(values, op):
        return op(values.T, axis=0, keepdims=True)

    def column(values, op, half):
        mine = jnp.where(core == half, values[:, :ROWS], values[:, ROWS:])
        return op(mine, axis=0, keepdims=True)

    def finish(tile):
        places = {0: SAME_CORE[tile]}
        if tile in COL_TILES:
            places[1] = CROSS_CORE[tile]
        for half, place in reversed(places.items()):
            sums = tops = None
            if tile in COL_TILES:
                sums = column(col_sums[tile], jnp.sum, half)
                tops = column(col_tops[tile], jnp.max, half)
            for at, (_, _, right) in enumerate(KEPT):
                if right is not None and right[0] == tile:
                    extra = column(col_sums[KEPT_COL + at], jnp.sum, half)
                    sums = sums + extra
                    tops = jnp.maximum(tops, column(col_tops[KEPT_COL + at], jnp.max, half))
                    if half == 0:
                        outbox[place, pl.ds(right[1], 1), :] = extra
            if half == 0 and (tile in ROW_TILES or tile == 0):
                if LANE_ROWS[tile] < ROUNDS:
                    low, high = row_lanes[tile, 0:1, :], row_lanes[tile, 1:2, :]
                else:
                    low, high = across(row_sums[tile], jnp.sum), across(row_tops[tile], jnp.max)
                sums = low if sums is None else sums + low
                tops = high if tops is None else jnp.maximum(tops, high)
                for at, (_, left, _) in enumerate(KEPT):
                    if left[0] == tile:
                        if LANE_KEPT[at] < ROUNDS:
                            kept = kept_lanes[at, 0:1, :]
                        else:
                            kept = across(kept_sums[at], jnp.sum)
                        outbox[place, pl.ds(left[1], 1), :] = kept
            outbox[place, 0:1, :] = sums
            outbox[place, 1:2, :] = tops
            if place != MESSAGES:
                post(tile, place, other if half else core).start()

    def lanes(row, kept):
        row_lanes[row, 0:1, :] = across(row_sums[row], jnp.sum)
        row_lanes[row, 1:2, :] = across(row_tops[row], jnp.max)
        kept_lanes[kept, 0:1, :] = across(kept_sums[kept], jnp.sum)

    def arrivals(number, second):
        if True:
            step = 2 * number + second
            if step < len(PAIRS):
                for tile, chunk in ARRIVALS[step]:
                    arrive(tile, chunk)
                for tile in SHARED_TILES:
                    if tile != 0 and first_use(tile) == step:
                        twin_whole(tile).wait_recv()
            values = slots(step) if step < len(PAIRS) else NOTHING
            if not second:
                row = [tile for tile, at in LANE_ROWS.items() if at == number] or [SPARE_ROW]
                kept = [place for place, at in LANE_KEPT.items() if at == number] or [SPARE_KEPT]
                values = values + (row[0], kept[0])
                for tile in range(COUNT):
                    if done_round(tile) == number:
                        finish(tile)
            return values

    before = NOTHING[2:5]
    for number in range(ROUNDS):
        one, two = arrivals(number, 0), arrivals(number, 1)
        lanes(*one[5:7])
        multiply(near, one[0], one[1])
        reduce(far, *before)
        multiply(far, two[0], two[1])
        reduce(near, *one[2:5])
        before = two[2:5]
    last = before
    reduce(far, *last)
    for tile in list(range(1, COUNT)) + [0]:
        if done_round(tile) == ROUNDS:
            finish(tile)
    table[0:1, :] = across(kept_sums[SPARE_KEPT + 1], jnp.sum)

    moved = tiles.at[pl.ds(1, COUNT - 1), core]
    pltpu.make_async_copy(moved, moved, hop_send).wait()
    shared = tiles.at[pl.ds(0, len(SHARED_TILES)), core]
    pltpu.make_async_copy(shared, shared, twin_send).wait()
    sent = outbox.at[pl.ds(0, MESSAGES)]
    pltpu.make_async_copy(sent, sent, post_send).wait()
    pltpu.make_async_copy(inbox, inbox, post_recv).wait()

    sums = tops = outbox[MESSAGES]
    for place in range(MESSAGES):
        sums = sums + inbox[place]
        tops = jnp.maximum(tops, inbox[place])
    total_ref[...] = sums
    high_ref[...] = tops
    for _, left, right in KEPT:
        for side in (left, right):
            if side is not None:
                where = outbox if side[0] == 0 else inbox
                table[pl.ds(side[2], 1), :] = where[SAME_CORE[side[0]], pl.ds(side[1], 1), :]

def finisher(cand_ref, total_ref, high_ref, table_ref, counts_ref, tops_ref, recount_ref):
    my_row = lax.axis_index("row")
    z, x_hi = my_row // 2, my_row % 2
    counts_ref[...] = total_ref[0, :]
    tops_ref[...] = high_ref[1, :]
    for number in range(2):
        chosen = cand_ref[number]
        apart = ((chosen // 2 - z + 4) % 4) * 2 + (chosen % 2 - x_hi + 2) % 2
        recount_ref[pl.ds(number, 1), :] = table_ref[pl.ds(apart, 1), :]


def per_device(embed, cand_tiles):
    vector = pltpu.VMEM
    semaphores = pltpu.SemaphoreType.DMA
    in_vector = pl.BlockSpec(memory_space=pltpu.VMEM)
    parts = pl.pallas_call(
        kernel,
        out_shape=(jax.ShapeDtypeStruct((8, ROWS), jnp.float32),) * 3,
        in_specs=[pl.BlockSpec(memory_space=pl.ANY)],
        out_specs=[in_vector] * 3,
        scratch_shapes=[
            vector((COUNT, 2, ROWS, WIDTH), jnp.bfloat16),
            vector((ROWS, 2 * ROWS), jnp.float32),
            vector((ROWS, 2 * ROWS), jnp.float32),
            vector((COUNT + 1, ROWS, 128), jnp.float32),
            vector((COUNT + 1, ROWS, 128), jnp.float32),
            vector((SPARE_KEPT + 2, ROWS, 128), jnp.float32),
            vector((KEPT_COL + len(KEPT), 8, 2 * ROWS), jnp.float32),
            vector((KEPT_COL + len(KEPT), 8, 2 * ROWS), jnp.float32),
            vector((COUNT + 1, 8, ROWS), jnp.float32),
            vector((SPARE_KEPT + 1, 8, ROWS), jnp.float32),
            vector((MESSAGES + 1, 8, ROWS), jnp.float32),
            vector((MESSAGES, 8, ROWS), jnp.float32),
            semaphores,
            semaphores,
            semaphores((COUNT, CHUNKS)),
            semaphores,
            semaphores((COUNT,)),
            semaphores,
            semaphores,
        ],
        compiler_params=pltpu.CompilerParams(
            collective_id=0, has_side_effects=True, vmem_limit_bytes=56 * 1024 * 1024
        ),
        cost_estimate=pl.CostEstimate(
            flops=37 * 2 * ROWS * 2 * ROWS * WIDTH,
            bytes_accessed=COUNT * 2 * ROWS * WIDTH * 2,
            transcendentals=37 * ROWS * 2 * ROWS,
        ),
    )(embed)
    return pl.pallas_call(
        finisher,
        out_shape=(
            jax.ShapeDtypeStruct((ROWS,), jnp.float32),
            jax.ShapeDtypeStruct((ROWS,), jnp.float32),
            jax.ShapeDtypeStruct((2, ROWS), jnp.float32),
        ),
        in_specs=[pl.BlockSpec(memory_space=pltpu.SMEM)] + [in_vector] * 3,
        out_specs=[in_vector] * 3,
    )(cand_tiles, *parts)


def solution(mesh):
    in_specs = (P(("row", "col"), None), P(("row", "col")))
    out_specs = (P(("row", "col")), P(("row", "col")), P(("row", "col"), None))
    return jax.shard_map(
        per_device, mesh=mesh, in_specs=in_specs, out_specs=out_specs, check_vma=False
    )
```
